256 devices in a mesh: seg: 64 (over y, z, core), head: 4 (over x).
Axes of the slice: x: 4, y: 4, z: 8, core: 2. Of those that a mesh axis runs over, the one named last changes fastest.
Arguments:
- queries: bfloat16 [16384, 2048], P('seg', 'head'), may hold values from -20 to 20
- keys: bfloat16 [16384, 2048], P('seg', 'head'), may hold values from -12 to 12
- values: bfloat16 [16384, 2048], P('seg', 'head'), may hold values from -6 to 6
- out_grad: bfloat16 [16384, 2048], P('seg', 'head'), may hold values from -5 to 5
- out_weight: bfloat16 [2048, 2048], P('head'), may hold values from -1 to 1
- retr_owner: int32 [64, 32], replicated, may hold values from 0 to 63, as said below
- retr_block: int32 [64, 32], replicated, may hold values from -1 to 1, as said below
Outputs:
- layer_out: bfloat16 [16384, 2048], P('seg', 'head')
- query_grad: bfloat16 [16384, 2048], P('seg', 'head')
- key_grad: bfloat16 [16384, 2048], P('seg', 'head')
- value_grad: bfloat16 [16384, 2048], P('seg', 'head')
- proj_grad_t: float32 [2048, 2048], P('seg', 'head')
The draws below stay inside these ranges and needn't reach their ends.
Inputs may be any that keep to these rules, and one draw needn't show every extreme that they name: `retr_owner`: row s lists 32 owners, all different from one another and from s. `retr_block`: padding (-1) comes after the live entries of a row; every row has at least 24 live entries.
All inputs are finite; a program needn't handle non-finite values.
Results may differ from the reference program's by a relative error of at most 0.012.
Values may be sent and summed in bfloat16 or wider, within the bound.
A program may use at most 128 MiB of HBM per device.

```python
import math
import jax
import jax.numpy as jnp
from jax import lax

D = 2048
HEADS = 16
DH = 128
BLOCK = 128
SEG = 256
SEGMENTS = 64
TOKENS = 16384
MEMB = 2
R = 32


def draw_queries(key, part):
    spread = 2.0 * jnp.clip(jax.random.normal(jax.random.fold_in(key, 1), (TOKENS, HEADS * DH), jnp.float32), -6.0, 6.0)
    return spread.astype(jnp.bfloat16)


def draw_keys(key, part):
    spread = jnp.clip(jax.random.normal(jax.random.fold_in(key, 2), (TOKENS, HEADS * DH), jnp.float32), -6.0, 6.0)
    return spread.astype(jnp.bfloat16)


def draw_retr_owner(key, part):
    streams = jax.random.split(jax.random.fold_in(key, 5), SEGMENTS)
    orders = jax.vmap(lambda stream: jax.random.permutation(stream, SEGMENTS - 1))(streams)[:, :R]
    return ((jnp.arange(SEGMENTS)[:, None] + 1 + orders) % SEGMENTS).astype(jnp.int32)


def draw_retr_block(key, part):
    first_key, second_key = jax.random.split(jax.random.fold_in(key, 7))
    blocks = jax.random.randint(first_key, (SEGMENTS, R), 0, MEMB)
    blocks = blocks.at[0, 0].set(MEMB - 1)
    live_count = jax.random.randint(second_key, (SEGMENTS,), R - R // 4, R + 1)
    live_count = live_count.at[0].set(R).at[1].set(R - R // 4)
    places = jnp.arange(R)
    return jnp.where(places[None, :] < live_count[:, None], blocks, -1).astype(jnp.int32)


def spiked(array, key, source, target, shards_of, factor):
    def block_of(dim):
        return (jnp.arange(array.shape[dim]) // (array.shape[dim] // shards_of)).reshape((-1,) + (1,) * (array.ndim - 1 - dim))

    first = jax.random.permutation(key, shards_of)[block_of(target)]
    far = (block_of(target) + shards_of // 2) % shards_of
    return jnp.where((block_of(source) == first) | (block_of(source) == far), factor * array, array)


def block_scale(key, shape, cuts, low, high):
    gain = 1.0
    for axis_at, parts in cuts:
        heights = jax.random.uniform(jax.random.fold_in(jax.random.fold_in(key, 6), axis_at), (parts,), jnp.float32, low / len(cuts), high / len(cuts))
        gain = gain * jnp.repeat(jnp.exp(heights), shape[axis_at] // parts).reshape((-1,) + (1,) * (len(shape) - 1 - axis_at))
    return gain


def scatter_about(rng, shape, deviation, bound, pieces=(), kind=jnp.bfloat16):
    entries = jax.random.normal(rng, shape, jnp.float32) * deviation
    if len(pieces) > 0:
        entries = block_scale(rng, shape, pieces, -0.22, 0.18) * entries
    return jnp.clip(entries, min=-bound, max=bound).astype(kind)


def gaussian_with(stream_key, extent, scale, bound, cuts, heavy, held_as=jnp.bfloat16):
    values = scale * jax.random.normal(stream_key, extent, jnp.float32)
    if cuts:
        values = values * block_scale(stream_key, extent, cuts, -0.22, 0.18)
    return jnp.clip(spiked(values, jax.random.fold_in(stream_key, 3), *heavy), -bound, bound).astype(held_as)


def setup_inputs(seed: int = 0) -> dict:
    splits = jax.random.split(jax.random.key(seed), 8)
    return {
        "queries": draw_queries(jax.random.fold_in(splits[7], 71), 0),
        "keys": draw_keys(jax.random.fold_in(splits[7], 71), 0),
        "values": scatter_about(splits[2], (TOKENS, HEADS * DH), 1.0, 6.0, ((0, 64), (1, 4))),
        "out_grad": gaussian_with(splits[3], (TOKENS, D), 0.125, 5.0, ((0, 64), (1, 4)), (0, 1, 64, 4.0)),
        "out_weight": scatter_about(splits[4], (HEADS * DH, D), (DH // 4) ** -0.5, 1.0, ((0, 4),)),
        "retr_owner": draw_retr_owner(jax.random.fold_in(splits[7], 71), 0),
        "retr_block": draw_retr_block(jax.random.fold_in(splits[7], 71), 0),
    }


def split_heads(tok_rows, count):
    return tok_rows.reshape(tok_rows.shape[0], count, -1).transpose(1, 0, 2)

def join_heads(stacked):
    return stacked.transpose(1, 0, 2).reshape(stacked.shape[1], -1)

def product(form, left_side, right_side):
    return jnp.einsum(form, left_side.astype(jnp.float32), right_side.astype(jnp.float32))

def attend(queries, keys, values, cache_k, cache_v, mem_k, mem_v, mem_live, has_cache, d_attn, score_scale):
    length = queries.shape[1]
    causal = jnp.arange(length)[:, None] >= jnp.arange(length)[None, :]
    own = jnp.where(causal[None], product('hqd,hkd->hqk', queries, keys) * score_scale, -jnp.inf)
    cached = jnp.where(has_cache, product('hqd,hkd->hqk', queries, cache_k) * score_scale, -jnp.inf)
    stored = jnp.where(mem_live[None, None, :], product('hqd,hkd->hqk', queries, mem_k) * score_scale, -jnp.inf)
    row_top = jnp.maximum(jnp.maximum(lax.optimization_barrier(jnp.max(own, -1)), lax.optimization_barrier(jnp.max(cached, -1))), lax.optimization_barrier(jnp.max(stored, -1)))[..., None]
    row_total = lax.optimization_barrier(jnp.sum(jnp.exp(own - row_top), -1)) + lax.optimization_barrier(jnp.sum(jnp.exp(cached - row_top), -1)) + lax.optimization_barrier(jnp.sum(jnp.exp(stored - row_top), -1))
    log_total = row_top + jnp.log(row_total)[..., None]
    weights = [jnp.exp(group_scores - log_total) for group_scores in (own, cached, stored)]
    rounded = [entry.astype(jnp.bfloat16) for entry in weights]
    sources = (values, cache_v, mem_v)
    mixed_sum = product('hqk,hkd->hqd', rounded[0], sources[0]) + product('hqk,hkd->hqd', rounded[1], sources[1]) + product('hqk,hkd->hqd', rounded[2], sources[2])
    attn = mixed_sum.astype(jnp.bfloat16)
    row_delta = lax.optimization_barrier(jnp.sum(d_attn.astype(jnp.float32) * attn.astype(jnp.float32), -1))[..., None]
    slopes = [(entry * (product('hqd,hkd->hqk', d_attn, source) - row_delta)).astype(jnp.bfloat16) for entry, source in zip(weights, sources)]
    grad_q = score_scale * (product('hqk,hkd->hqd', slopes[0], keys) + product('hqk,hkd->hqd', slopes[1], cache_k) + product('hqk,hkd->hqd', slopes[2], mem_k))
    grad_k_own = score_scale * product('hqk,hqd->hkd', slopes[0], queries)
    grad_v_own = product('hqk,hqd->hkd', rounded[0], d_attn)
    grad_k_cache = score_scale * product('hqk,hqd->hkd', slopes[1], queries)
    grad_v_cache = product('hqk,hqd->hkd', rounded[1], d_attn)
    return (attn, grad_q, grad_k_own, grad_v_own, grad_k_cache, grad_v_cache)

def reference(queries, keys, values, out_grad, out_weight, retr_owner, retr_block):
    score_scale = 1.0 / math.sqrt(DH)
    d_attn = jnp.dot(out_grad, out_weight.T, preferred_element_type=jnp.float32).astype(jnp.bfloat16)
    offsets = jnp.arange(BLOCK, dtype=jnp.int32)

    def one_segment(segment):

        def rows_at(source, begin):
            return split_heads(lax.dynamic_slice_in_dim(source, begin, SEG, 0), HEADS)
        start = (segment * SEG).astype(jnp.int32)
        previous = (jnp.maximum(segment - 1, 0) * SEG).astype(jnp.int32)
        owners = retr_owner[segment]
        blocks = retr_block[segment]
        picked = ((owners * SEG + jnp.maximum(blocks, 0) * BLOCK)[:, None] + offsets[None, :]).reshape(-1).astype(jnp.int32)
        mem_k = split_heads(keys[picked], HEADS)
        mem_v = split_heads(values[picked], HEADS)
        mem_live = jnp.repeat(blocks >= 0, BLOCK)
        results = attend(rows_at(queries, start), rows_at(keys, start), rows_at(values, start), rows_at(keys, previous), rows_at(values, previous), mem_k, mem_v, mem_live, segment > 0, rows_at(d_attn, start), score_scale)
        return tuple((join_heads(entry) for entry in results))
    attn, grad_q, grad_k_own, grad_v_own, grad_k_cache, grad_v_cache = lax.map(one_segment, jnp.arange(SEGMENTS, dtype=jnp.int32))
    carried_k = jnp.concatenate([grad_k_cache[1:], jnp.zeros_like(grad_k_cache[:1])], 0)
    carried_v = jnp.concatenate([grad_v_cache[1:], jnp.zeros_like(grad_v_cache[:1])], 0)
    attn_rows = attn.reshape(TOKENS, -1)
    layer_out = jnp.dot(attn_rows, out_weight, preferred_element_type=jnp.float32).astype(jnp.bfloat16)
    query_grad = grad_q.reshape(TOKENS, -1).astype(jnp.bfloat16)
    key_grad = (grad_k_own + carried_k).reshape(TOKENS, -1).astype(jnp.bfloat16)
    value_grad = (grad_v_own + carried_v).reshape(TOKENS, -1).astype(jnp.bfloat16)
    proj_grad_t = jnp.dot(out_grad.T, attn_rows, preferred_element_type=jnp.float32)
    return (layer_out, query_grad, key_grad, value_grad, proj_grad_t)
```

```python
import math

import jax
import jax.numpy as jnp
from jax import lax
from jax.experimental import pallas as pl
from jax.experimental.pallas import tpu as pltpu
from jax.sharding import PartitionSpec as P

DH = 128
BLOCK = 128
SEG = 256
R = 32
NY, NZ, NC, NX = 4, 8, 2, 4
MESH = pl.DeviceIdType.MESH
F32, BF16 = jnp.float32, jnp.bfloat16
NEG = -1e30
SURE = 24
PER = 4
WIDE = PER * BLOCK
CHUNKS = R // PER


def dot_nt(a, b):
    return lax.dot_general(a, b, (((1,), (1,)), ((), ())), preferred_element_type=F32)


def dot_nn(a, b):
    return lax.dot_general(a, b, (((1,), (0,)), ((), ())), preferred_element_type=F32)


def dot_tn(a, b):
    return lax.dot_general(a, b, (((0,), (0,)), ((), ())), preferred_element_type=F32)


def kernel(
    owner_ref, block_ref, q_ref, k_ref, v_ref, g_ref, w_ref,
    lo_ref, dq_ref, dk_ref, dv_ref, pg_ref,
    kv, q4, do4, dal, fg, s_mem, s_near, p_mem, stat, attn4, attn_in, lo_out, lo_in,
    pp, rs0, r1, rs1, r2, rs2, dq_acc, near_acc, carry_out, carry_in, gq, gk, gv,
    loc, ys, yr, xs, xr, zs, zr, ms, mr, ds_, dr, as_, ar, cs, cr, bs, br, rys, ryr, rzs, rzr, ls, lr, os_, or_,
):
    s_me = lax.axis_index("seg")
    x = lax.axis_index("head")
    c = lax.rem(s_me, NC)
    z = lax.rem(lax.div(s_me, NC), NZ)
    y = lax.div(s_me, NC * NZ)
    scale = 1.0 / math.sqrt(DH)
    scale2 = scale * math.log2(math.e)

    def seg_of(yy, zz, cc):
        return (yy * NZ + zz) * NC + cc

    y_of = [lax.rem(y + d, NY) for d in range(NY)]
    x_of = [lax.rem(x + d, NX) for d in range(NX)]
    z_of = [lax.rem(z + d, NZ) for d in range(NZ)]
    y_peer = [(seg_of(y_of[d], z, c), x) for d in range(NY)]
    z_peer = [(seg_of(y, z_of[d], c), x) for d in range(NZ)]
    x_peer = [(s_me, x_of[d]) for d in range(NX)]
    sibling = (seg_of(y, z, 1 - c), x)
    cross = (seg_of(y, lax.rem(z + NZ - 1 + 2 * c, NZ), 1 - c), x)
    back = (seg_of(y, lax.rem(z + NZ - 1 + c, NZ), 1 - c), x)
    wrap = 1 - jnp.minimum(z + c, 1)

    sends = []

    def send(src, dst, ssem, rsem, dev):
        copy = pltpu.make_async_remote_copy(
            src_ref=src, dst_ref=dst, send_sem=ssem, recv_sem=rsem, device_id=dev, device_id_type=MESH
        )
        copy.start()
        sends.append(copy)

    def arrived(dst, ssem, rsem):
        pltpu.make_async_remote_copy(
            src_ref=dst, dst_ref=dst, send_sem=ssem, recv_sem=rsem, device_id=sibling, device_id_type=MESH
        ).wait_recv()

    def cols(i):
        return pl.ds(pl.multiple_of(i * DH, DH), DH)

    def slot(plane, rz, ry):
        return (plane * NZ + rz) * NY + ry

    own = [
        pltpu.make_async_copy(k_ref.at[:, :, cols(y)], kv.at[0, 0], loc.at[0]),
        pltpu.make_async_copy(v_ref.at[:, :, cols(y)], kv.at[0, 1], loc.at[1]),
        pltpu.make_async_copy(q_ref.at[:, cols(y)], q4.at[0], loc.at[2]),
        pltpu.make_async_copy(g_ref, fg.at[x], loc.at[3]),
    ]
    for copy in own:
        copy.start()

    barrier = pltpu.get_barrier_semaphore()
    peers = y_peer[1:] + z_peer[1:] + x_peer[1:] + [sibling, cross]
    for dev in peers:
        pl.semaphore_signal(barrier, inc=1, device_id=dev, device_id_type=MESH)
    pl.semaphore_wait(barrier, len(peers))

    for d in (1, 3, 2):
        send(k_ref.at[:, :, cols(y_of[d])], kv.at[NY - d, 0], ys.at[d - 1, 0], yr.at[NY - d - 1, 0], y_peer[d])
        send(v_ref.at[:, :, cols(y_of[d])], kv.at[NY - d, 1], ys.at[d - 1, 1], yr.at[NY - d - 1, 1], y_peer[d])
    for d in (1, 3, 2):
        send(g_ref, fg.at[x], xs.at[d - 1], xr.at[d - 1], x_peer[d])
    for copy in own:
        copy.wait()
    order = (0, 1, 3, 2)

    def z_step(t):
        up, down = (NZ - t) % NZ, t
        for ry in order:
            if t == 0:
                if ry:
                    arrived(kv.at[ry, 0], ys.at[ry - 1, 0], yr.at[ry - 1, 0])
                    arrived(kv.at[ry, 1], ys.at[ry - 1, 1], yr.at[ry - 1, 1])
            else:
                arrived(kv.at[slot(0, up, ry)], zs.at[0, t - 1, ry], zr.at[0, t - 1, ry])
                arrived(kv.at[slot(0, down, ry)], zs.at[1, t - 1, ry], zr.at[1, t - 1, ry])
            if t < NZ // 2 - 1:
                send(kv.at[slot(0, up, ry)], kv.at[slot(0, NZ - 1 - t, ry)], zs.at[0, t, ry], zr.at[0, t, ry], z_peer[1])
                send(kv.at[slot(0, down, ry)], kv.at[slot(0, t + 1, ry)], zs.at[1, t, ry], zr.at[1, t, ry], z_peer[NZ - 1])
            else:
                far = slot(0, NZ // 2, ry)
                send(kv.at[slot(0, up, ry), 0], kv.at[far, 0], zs.at[0, t, ry], zr.at[0, t, ry], z_peer[1])
                send(kv.at[slot(0, down, ry), 1], kv.at[far, 1], zs.at[1, t, ry], zr.at[1, t, ry], z_peer[NZ - 1])
            for rz in ((0,) if t == 0 else (up, down)):
                send(kv.at[slot(0, rz, ry)], kv.at[slot(1, rz, ry)], ms.at[rz, ry], mr.at[rz, ry], sibling)

    z_step(0)
    for d in (1, 3, 2):
        send(q_ref.at[:, cols(y_of[d])], q4.at[NY - d], ys.at[d - 1, 2], yr.at[NY - d - 1, 2], y_peer[d])

    for d in (1, 3, 2):
        arrived(fg.at[x_of[NX - d]], xs.at[d - 1], xr.at[d - 1])
    width = g_ref.shape[1]
    da = dot_nt(fg[0], w_ref[:, :width])
    for i in range(1, NX):
        da += dot_nt(fg[i], w_ref[:, i * width : (i + 1) * width])
    da = da.astype(BF16)
    for i in range(NY):
        dal[i] = da[:, i * DH : (i + 1) * DH]
    do4[0] = dal[y]
    for d in (1, 3, 2):
        send(dal.at[y_of[d]], do4.at[NY - d], ds_.at[d - 1], dr.at[NY - d - 1], y_peer[d])

    for t in range(1, NZ // 2):
        z_step(t)
    for ry in order:
        far = slot(0, NZ // 2, ry)
        t = NZ // 2 - 1
        arrived(kv.at[far, 0], zs.at[0, t, ry], zr.at[0, t, ry])
        arrived(kv.at[far, 1], zs.at[1, t, ry], zr.at[1, t, ry])
        send(kv.at[far], kv.at[slot(1, NZ // 2, ry)], ms.at[NZ // 2, ry], mr.at[NZ // 2, ry], sibling)
    for ry in range(1, NY):
        arrived(q4.at[ry], ys.at[ry - 1, 2], yr.at[ry - 1, 2])
        arrived(do4.at[ry], ds_.at[ry - 1], dr.at[ry - 1])
    for rz in range(NZ):
        for ry in range(NY):
            arrived(kv.at[slot(1, rz, ry)], ms.at[rz, ry], mr.at[rz, ry])

    causal = lax.broadcasted_iota(jnp.int32, (SEG, SEG), 0) >= lax.broadcasted_iota(jnp.int32, (SEG, SEG), 1)

    def seg_id(ry):
        return seg_of(lax.rem(y + ry, NY), z, c)

    def cache_slot(ry):
        return slot(1, (NZ - 1) * (1 - c), lax.rem(ry + NY - wrap, NY))

    def place(ry, j):
        o = owner_ref[seg_id(ry), j]
        b = jnp.maximum(block_ref[seg_id(ry), j], 0)
        oc = lax.rem(o, NC)
        oz = lax.rem(lax.div(o, NC), NZ)
        oy = lax.div(o, NC * NZ)
        plane = lax.rem(oc + c, NC)
        rz = lax.rem(oz + NZ - z, NZ)
        return slot(plane, rz, lax.rem(oy + NY - y, NY)), b

    def stored(ry, i, which):
        parts = []
        for b in range(PER):
            at, half = place(ry, i * PER + b)
            parts.append(kv[at, which, half])
        return jnp.concatenate(parts, axis=0)

    def near(ref_at, which):
        return kv[ref_at, which].reshape(SEG, DH)

    def fold(m, entry, op):
        for i in range(entry.shape[1] // DH):
            m = op(m, entry[:, i * DH : (i + 1) * DH])
        return m

    def forward(ry):
        q = q4[ry]
        s_own = jnp.where(causal, dot_nt(q, near(ry, 0)), NEG)
        s_near[ry, 0] = s_own
        top = fold(s_own[:, :DH], s_own[:, DH:], jnp.maximum)
        has_cache = jnp.minimum(seg_id(ry), 1).astype(F32)
        s_cache = dot_nt(q, near(cache_slot(ry), 0)) + (1.0 - has_cache) * NEG
        s_near[ry, 1] = s_cache
        top = fold(top, s_cache, jnp.maximum)

        def score(i, top, sure):
            s = dot_nt(q, stored(ry, i, 0))
            if not sure:
                parts = []
                for b in range(PER):
                    dead = jnp.maximum(-block_ref[seg_id(ry), i * PER + b], 0).astype(F32)
                    parts.append(s[:, b * BLOCK : (b + 1) * BLOCK] + dead * NEG)
                s = jnp.concatenate(parts, axis=1)
            s_mem[i] = s
            return fold(top, s, jnp.maximum)

        top = lax.fori_loop(0, SURE // PER, lambda i, m: score(i, m, True), top)
        top = lax.fori_loop(SURE // PER, CHUNKS, lambda i, m: score(i, m, False), top)
        top = jnp.max(top, axis=1, keepdims=True)
        total = jnp.zeros((SEG, DH), F32)
        mixed = jnp.zeros((SEG, DH), F32)
        for part, at in ((0, ry), (1, cache_slot(ry))):
            p = jnp.exp2((s_near[ry, part] - top) * scale2)
            total = fold(total, p, jnp.add)
            mixed += dot_nn(p.astype(BF16), near(at, 1))

        def mix(i, held):
            total, mixed = held
            p = jnp.exp2((s_mem[i] - top) * scale2)
            total = fold(total, p, jnp.add)
            p = p.astype(BF16)
            p_mem[ry, i] = p
            return total, mixed + dot_nn(p, stored(ry, i, 1))

        total, mixed = lax.fori_loop(0, CHUNKS, mix, (total, mixed))
        inv = 1.0 / jnp.sum(total, axis=1, keepdims=True)
        attn = (mixed * inv).astype(BF16)
        attn4[ry] = attn
        delta = jnp.sum(do4[ry].astype(F32) * attn.astype(F32), axis=1, keepdims=True)
        stat[ry, 0] = jnp.broadcast_to(top, (SEG, DH))
        stat[ry, 1] = jnp.broadcast_to(inv, (SEG, DH))
        stat[ry, 2] = jnp.broadcast_to(delta, (SEG, DH))

    def backward_near(ry):
        q, do = q4[ry], do4[ry]
        top, inv, delta = stat[ry, 0, :, :1], stat[ry, 1, :, :1], stat[ry, 2, :, :1]
        dq = jnp.zeros((SEG, DH), F32)
        for part, at in ((0, ry), (1, cache_slot(ry))):
            weights = jnp.exp2((s_near[ry, part] - top) * scale2) * inv
            slopes = (weights * (dot_nt(do, near(at, 1)) - delta)).astype(BF16)
            dq += dot_nn(slopes, near(at, 0))
            gk_part = dot_tn(slopes, q) * scale
            gv_part = dot_tn(weights.astype(BF16), do)
            if part == 0:
                near_acc[ry, 0] = gk_part
                near_acc[ry, 1] = gv_part
            else:
                carry_out[ry, 0] = gk_part.astype(BF16)
                carry_out[ry, 1] = gv_part.astype(BF16)
        dq_acc[ry] = dq

    def backward_mem(ry):
        do = do4[ry]
        inv, delta = stat[ry, 1, :, :1], stat[ry, 2, :, :1]

        def step(i, dq):
            slopes = (p_mem[ry, i].astype(F32) * (dot_nt(do, stored(ry, i, 1)) - delta)).astype(BF16)
            return dq + dot_nn(slopes, stored(ry, i, 0))

        dq = lax.fori_loop(0, CHUNKS, step, jnp.zeros((SEG, DH), F32))
        gq[ry] = ((dq_acc[ry] + dq * inv) * scale).astype(BF16)

    for ry in range(NY):
        forward(ry)
        if ry:
            send(attn4.at[ry], attn_in.at[y], as_.at[ry - 1], ar.at[ry - 1], y_peer[ry])
    attn_in[y] = attn4[0]

    for ry in range(NY):
        backward_near(ry)
        to = lax.rem(ry + NY - wrap, NY)
        send(carry_out.at[ry], carry_in.at[to], cs.at[ry], cr.at[to], back)

    for d in range(1, NY):
        arrived(attn_in.at[y_of[NY - d]], as_.at[d - 1], ar.at[d - 1])
    attn = jnp.concatenate([attn_in[i] for i in range(NY)], axis=1)
    wide = attn.shape[1]
    rows = pg_ref.shape[0]
    for i in range(NY):
        part = dot_tn(fg[i], attn).reshape(NZ, NC, rows, wide)
        pp[i] = part.astype(BF16)
        send(pp.at[i, :, 1 - c], rs0.at[i], bs.at[i], br.at[i], sibling)
    for i in range(NX):
        lo_out[i] = dot_nn(attn, w_ref[:, i * width : (i + 1) * width]).astype(BF16)
    for d in (1, 3, 2):
        send(lo_out.at[x_of[d]], lo_in.at[d - 1], ls.at[d - 1], lr.at[d - 1], x_peer[d])

    backward_mem(0)
    for i in range(NY):
        arrived(rs0.at[i], bs.at[i], br.at[i])
        r1[i] = (pp[i, :, c].astype(F32) + rs0[i].astype(F32)).astype(BF16)
    for d in (1, 3, 2):
        send(r1.at[y_of[d]], rs1.at[d - 1], rys.at[d - 1], ryr.at[d - 1], y_peer[d])
    backward_mem(1)
    send(gq.at[1], dq_ref.at[:, cols(y)], os_.at[0, 0], or_.at[0, 0], y_peer[1])
    for ry in range(NY):
        arrived(carry_in.at[ry], cs.at[ry], cr.at[ry])
        gk[ry] = (near_acc[ry, 0] + carry_in[ry, 0].astype(F32)).astype(BF16)
        gv[ry] = (near_acc[ry, 1] + carry_in[ry, 1].astype(F32)).astype(BF16)
        if ry:
            send(gk.at[ry], dk_ref.at[:, cols(y)], os_.at[1, ry - 1], or_.at[1, ry - 1], y_peer[ry])
            send(gv.at[ry], dv_ref.at[:, cols(y)], os_.at[2, ry - 1], or_.at[2, ry - 1], y_peer[ry])
    backward_mem(2)
    send(gq.at[2], dq_ref.at[:, cols(y)], os_.at[0, 1], or_.at[0, 1], y_peer[2])
    total = r1[y].astype(F32)
    for d in range(1, NY):
        arrived(rs1.at[d - 1], rys.at[d - 1], ryr.at[d - 1])
        total += rs1[d - 1].astype(F32)
    r2[...] = total.astype(BF16)
    for d in range(1, NZ):
        send(r2.at[z_of[d]], rs2.at[d - 1], rzs.at[d - 1], rzr.at[d - 1], z_peer[d])
    backward_mem(3)
    send(gq.at[3], dq_ref.at[:, cols(y)], os_.at[0, 2], or_.at[0, 2], y_peer[3])

    home = [
        pltpu.make_async_copy(gq.at[0], dq_ref.at[:, cols(y)], loc.at[0]),
        pltpu.make_async_copy(gk.at[0], dk_ref.at[:, cols(y)], loc.at[1]),
        pltpu.make_async_copy(gv.at[0], dv_ref.at[:, cols(y)], loc.at[2]),
    ]
    for copy in home:
        copy.start()
    out = lo_out[x].astype(F32)
    for d in range(1, NX):
        arrived(lo_in.at[d - 1], ls.at[d - 1], lr.at[d - 1])
        out += lo_in[d - 1].astype(F32)
    lo_ref[...] = out.astype(BF16)
    total = r2[z].astype(F32)
    for d in range(1, NZ):
        arrived(rs2.at[d - 1], rzs.at[d - 1], rzr.at[d - 1])
        total += rs2[d - 1].astype(F32)
    pg_ref[...] = total
    for n, ref in enumerate((dq_ref, dk_ref, dv_ref)):
        for d in range(1, NY):
            arrived(ref.at[:, cols(y_of[NY - d])], os_.at[n, d - 1], or_.at[n, d - 1])
    for copy in home:
        copy.wait()
    for copy in sends:
        copy.wait_send()


def per_device(queries, keys, values, out_grad, out_weight, retr_owner, retr_block):
    tok, wide = queries.shape
    full = out_weight.shape[1]
    rows = full // (NY * NZ * NC)
    vmem = pl.BlockSpec(memory_space=pltpu.VMEM)
    smem = pl.BlockSpec(memory_space=pltpu.SMEM)
    dma = pltpu.SemaphoreType.DMA
    tile = (tok, DH)
    halves = tok // BLOCK
    scratch = [
        pltpu.VMEM((NC * NZ * NY, 2, halves, BLOCK, DH), BF16),
        pltpu.VMEM((NY,) + tile, BF16),
        pltpu.VMEM((NY,) + tile, BF16),
        pltpu.VMEM((NY,) + tile, BF16),
        pltpu.VMEM((NX, tok, wide), BF16),
        pltpu.VMEM((CHUNKS, tok, WIDE), F32),
        pltpu.VMEM((NY, 2, tok, tok), F32),
        pltpu.VMEM((NY, CHUNKS, tok, WIDE), BF16),
        pltpu.VMEM((NY, 3) + tile, F32),
        pltpu.VMEM((NY,) + tile, BF16),
        pltpu.VMEM((NY,) + tile, BF16),
        pltpu.VMEM((NX, tok, wide), BF16),
        pltpu.VMEM((NX - 1, tok, wide), BF16),
        pltpu.VMEM((NY, NZ, NC, rows, wide), BF16),
        pltpu.VMEM((NY, NZ, rows, wide), BF16),
        pltpu.VMEM((NY, NZ, rows, wide), BF16),
        pltpu.VMEM((NY - 1, NZ, rows, wide), BF16),
        pltpu.VMEM((NZ, rows, wide), BF16),
        pltpu.VMEM((NZ - 1, rows, wide), BF16),
        pltpu.VMEM((NY,) + tile, F32),
        pltpu.VMEM((NY, 2) + tile, F32),
        pltpu.VMEM((NY, 2) + tile, BF16),
        pltpu.VMEM((NY, 2) + tile, BF16),
        pltpu.VMEM((NY,) + tile, BF16),
        pltpu.VMEM((NY,) + tile, BF16),
        pltpu.VMEM((NY,) + tile, BF16),
        dma((4,)),
        dma((NY - 1, 3)), dma((NY - 1, 3)),
        dma((NX - 1,)), dma((NX - 1,)),
        dma((2, NZ // 2, NY)), dma((2, NZ // 2, NY)),
        dma((NZ, NY)), dma((NZ, NY)),
        dma((NY - 1,)), dma((NY - 1,)),
        dma((NY - 1,)), dma((NY - 1,)),
        dma((NY,)), dma((NY,)),
        dma((NY,)), dma((NY,)),
        dma((NY - 1,)), dma((NY - 1,)),
        dma((NZ - 1,)), dma((NZ - 1,)),
        dma((NX - 1,)), dma((NX - 1,)),
        dma((3, NY - 1)), dma((3, NY - 1)),
    ]
    grad = jax.ShapeDtypeStruct((tok, wide), BF16)
    return pl.pallas_call(
        kernel,
        out_shape=(grad, grad, grad, grad, jax.ShapeDtypeStruct((rows, wide), F32)),
        in_specs=[smem, smem] + [vmem] * 5,
        out_specs=(vmem,) * 5,
        scratch_shapes=scratch,
        compiler_params=pltpu.CompilerParams(
            collective_id=0, has_side_effects=True, vmem_limit_bytes=60 * 1024 * 1024
        ),
    )(
        retr_owner,
        retr_block,
        queries,
        keys.reshape(halves, BLOCK, wide),
        values.reshape(halves, BLOCK, wide),
        out_grad,
        out_weight,
    )


def solution(mesh):
    rows = P("seg", "head")
    return jax.shard_map(
        per_device,
        mesh=mesh,
        in_specs=(rows, rows, rows, rows, P("head", None), P(), P()),
        out_specs=(rows,) * 5,
        check_vma=False,
    )
```

```python
import math

import jax
import jax.numpy as jnp
from jax import lax
from jax.experimental import pallas as pl
from jax.experimental.pallas import tpu as pltpu
from jax.sharding import PartitionSpec as P

DH = 128
BLOCK = 128
SEG = 256
R = 32
NY, NZ, NC, NX = 4, 8, 2, 4
MESH = pl.DeviceIdType.MESH
F32, BF16 = jnp.float32, jnp.bfloat16
NEG = -1e30
SURE = 24
PER = 4
WIDE = PER * BLOCK
CHUNKS = R // PER


def dot_nt(a, b):
    return lax.dot_general(a, b, (((1,), (1,)), ((), ())), preferred_element_type=F32)


def dot_nn(a, b):
    return lax.dot_general(a, b, (((1,), (0,)), ((), ())), preferred_element_type=F32)


def dot_tn(a, b):
    return lax.dot_general(a, b, (((0,), (0,)), ((), ())), preferred_element_type=F32)


def kernel(
    owner_ref, block_ref, q_ref, k_ref, v_ref, g_ref, w_ref,
    lo_ref, dq_ref, dk_ref, dv_ref, pg_ref,
    kv, kvc, q4, do4, dal, fg, fgt, s_near, p_mem, m_mem, top4, sum4, mix4, stat, attn4, attn_in, lo_out, lo_in,
    pp, rs0, r1, ra, rb, ra_out, rb_out, ra2, rb2, r2, rs2, dq_acc, near_acc, carry_out, carry_in, gq, gk, gv,
    tab_v, tab,
    loc, ys, yr, xs, xr, zs, zr, ms, mr, ds_, dr, as_, ar, cs, cr, bs, br, rys, ryr, rzs, rzr, ls, lr, os_, or_,
):
    s_me = lax.axis_index("seg")
    x = lax.axis_index("head")
    c = lax.rem(s_me, NC)
    z = lax.rem(lax.div(s_me, NC), NZ)
    y = lax.div(s_me, NC * NZ)
    scale = 1.0 / math.sqrt(DH)
    scale2 = scale * math.log2(math.e)

    def seg_of(yy, zz, cc):
        return (yy * NZ + zz) * NC + cc

    y_of = [lax.rem(y + d, NY) for d in range(NY)]
    x_of = [lax.rem(x + d, NX) for d in range(NX)]
    z_of = [lax.rem(z + d, NZ) for d in range(NZ)]
    y_peer = [(seg_of(y_of[d], z, c), x) for d in range(NY)]
    z_peer = [(seg_of(y, z_of[d], c), x) for d in range(NZ)]
    x_peer = [(s_me, x_of[d]) for d in range(NX)]
    sibling = (seg_of(y, z, 1 - c), x)
    cross = (seg_of(y, lax.rem(z + NZ - 1 + 2 * c, NZ), 1 - c), x)
    back = (seg_of(y, lax.rem(z + NZ - 1 + c, NZ), 1 - c), x)
    wrap = 1 - jnp.minimum(z + c, 1)

    sends = []

    def send(src, dst, ssem, rsem, dev):
        copy = pltpu.make_async_remote_copy(
            src_ref=src, dst_ref=dst, send_sem=ssem, recv_sem=rsem, device_id=dev, device_id_type=MESH
        )
        copy.start()
        sends.append(copy)

    def arrived(dst, ssem, rsem):
        pltpu.make_async_remote_copy(
            src_ref=dst, dst_ref=dst, send_sem=ssem, recv_sem=rsem, device_id=sibling, device_id_type=MESH
        ).wait_recv()

    def cols(i):
        return pl.ds(pl.multiple_of(i * DH, DH), DH)

    def slot(plane, rz, ry):
        return (plane * NZ + rz) * NY + ry

    own = [
        pltpu.make_async_copy(k_ref.at[:, :, cols(y)], kv.at[0, 0], loc.at[0]),
        pltpu.make_async_copy(v_ref.at[:, :, cols(y)], kv.at[0, 1], loc.at[1]),
        pltpu.make_async_copy(q_ref.at[:, cols(y)], q4.at[0], loc.at[2]),
        pltpu.make_async_copy(g_ref, fg.at[x], loc.at[3]),
    ]
    for copy in own:
        copy.start()

    barrier = pltpu.get_barrier_semaphore()
    peers = y_peer[1:] + z_peer[1:] + x_peer[1:] + [sibling, cross]
    for dev in peers:
        pl.semaphore_signal(barrier, inc=1, device_id=dev, device_id_type=MESH)
    pl.semaphore_wait(barrier, len(peers))

    for d in (1, 3, 2):
        send(k_ref.at[:, :, cols(y_of[d])], kv.at[NY - d, 0], ys.at[d - 1, 0], yr.at[NY - d - 1, 0], y_peer[d])
        send(v_ref.at[:, :, cols(y_of[d])], kv.at[NY - d, 1], ys.at[d - 1, 1], yr.at[NY - d - 1, 1], y_peer[d])
    send(g_ref, fg.at[x], xs.at[0], xr.at[0], x_peer[1])
    send(g_ref, fg.at[x], xs.at[1], xr.at[1], x_peer[NX - 1])
    for copy in own:
        copy.wait()
    order = (0, 1, 3, 2)

    def z_part(t, ry):
        up, down = (NZ - t) % NZ, t
        if t == 0:
            if ry:
                arrived(kv.at[ry, 0], ys.at[ry - 1, 0], yr.at[ry - 1, 0])
                arrived(kv.at[ry, 1], ys.at[ry - 1, 1], yr.at[ry - 1, 1])
        else:
            arrived(kv.at[slot(0, up, ry)], zs.at[0, t - 1, ry], zr.at[0, t - 1, ry])
            arrived(kv.at[slot(0, down, ry)], zs.at[1, t - 1, ry], zr.at[1, t - 1, ry])
        if t < NZ // 2 - 1:
            send(kv.at[slot(0, up, ry)], kv.at[slot(0, NZ - 1 - t, ry)], zs.at[0, t, ry], zr.at[0, t, ry], z_peer[1])
            send(kv.at[slot(0, down, ry)], kv.at[slot(0, t + 1, ry)], zs.at[1, t, ry], zr.at[1, t, ry], z_peer[NZ - 1])
        else:
            far = slot(0, NZ // 2, ry)
            send(kv.at[slot(0, up, ry), 0], kv.at[far, 0], zs.at[0, t, ry], zr.at[0, t, ry], z_peer[1])
            send(kv.at[slot(0, down, ry), 1], kv.at[far, 1], zs.at[1, t, ry], zr.at[1, t, ry], z_peer[NZ - 1])
        for rz in ((0,) if t == 0 else (up, down)):
            send(kv.at[slot(0, rz, ry)], kv.at[slot(1, rz, ry)], ms.at[rz, ry], mr.at[rz, ry], sibling)

    def z_far(ry):
        far, t = slot(0, NZ // 2, ry), NZ // 2 - 1
        arrived(kv.at[far, 0], zs.at[0, t, ry], zr.at[0, t, ry])
        arrived(kv.at[far, 1], zs.at[1, t, ry], zr.at[1, t, ry])
        send(kv.at[far], kv.at[slot(1, NZ // 2, ry)], ms.at[NZ // 2, ry], mr.at[NZ // 2, ry], sibling)

    def take(rz, ry):
        arrived(kv.at[slot(1, rz, ry)], ms.at[rz, ry], mr.at[rz, ry])
        for plane in range(NC):
            kvc[slot(plane, rz, ry)] = kv[slot(plane, rz, ry)]

    def seg_id(ry):
        return seg_of(lax.rem(y + ry, NY), z, c)

    def cache_slot(ry):
        return slot(1, (NZ - 1) * (1 - c), lax.rem(ry + NY - wrap, NY))

    def near(at, which):
        return kvc[at, which].reshape(SEG, DH)

    def fold(m, entry, op):
        for i in range(entry.shape[1] // DH):
            m = op(m, entry[:, i * DH : (i + 1) * DH])
        return m

    def make_table(ry):
        lane = lax.broadcasted_iota(jnp.int32, owner_ref.shape, 1) == seg_id(ry)
        o = jnp.sum(jnp.where(lane, owner_ref[...], 0), axis=1, keepdims=True)
        b = jnp.sum(jnp.where(lane, block_ref[...], 0), axis=1, keepdims=True)
        rz = ((o >> 1) & (NZ - 1)) + NZ - z & (NZ - 1)
        rr = (o >> 4) + NY - y & (NY - 1)
        plane = (o + c) & (NC - 1)
        away = jnp.minimum(rz, NZ - rz)
        dead = b < 0
        turn = rr ^ (rr >> 1)
        stage = jnp.where(away < 3, 0, jnp.where(away == 3, 1 + turn, 1 + NY + turn))
        stage = jnp.where(dead, -1, stage)
        code = jnp.where(dead, 256, ((plane * NZ + rz) * NY + rr) * 2 + jnp.maximum(b, 0))
        down = lax.broadcasted_iota(jnp.int32, (R, R), 0)
        across = lax.broadcasted_iota(jnp.int32, (R, R), 1)
        stage_col = jnp.broadcast_to(stage, (R, R))
        stage_row = jnp.sum(jnp.where(down == across, stage_col, 0), axis=0, keepdims=True)
        first = (stage_row < stage_col) | ((stage_row == stage_col) & (across < down))
        rank = jnp.sum(first.astype(jnp.int32), axis=1, keepdims=True)
        tab_v[ry : ry + 1, :R] = jnp.sum(jnp.where(rank == across, code, 0), axis=0, keepdims=True)

    def stored(ry, i, which):
        parts = []
        for b in range(PER):
            code = tab[ry, i * PER + b]
            parts.append(kvc[(code & 255) >> 1, which, code & 1])
        return jnp.concatenate(parts, axis=0)

    causal = lax.broadcasted_iota(jnp.int32, (SEG, SEG), 0) >= lax.broadcasted_iota(jnp.int32, (SEG, SEG), 1)

    def forward_near(ry):
        q = q4[ry]
        s_own = jnp.where(causal, dot_nt(q, near(ry, 0)), NEG)
        s_near[ry, 0] = s_own
        dead = (1 - jnp.minimum(seg_id(ry), 1)).astype(F32)
        s_cache = dot_nt(q, near(cache_slot(ry), 0)) + dead * NEG
        s_near[ry, 1] = s_cache
        top = fold(fold(s_own[:, :DH], s_own[:, DH:], jnp.maximum), s_cache, jnp.maximum)
        top = jnp.broadcast_to(jnp.max(top, axis=1, keepdims=True), (SEG, DH))
        total = jnp.zeros((SEG, DH), F32)
        mixed = jnp.zeros((SEG, DH), F32)
        wide_top = jnp.concatenate([top] * (SEG // DH), axis=1)
        for s, at in ((s_own, ry), (s_cache, cache_slot(ry))):
            p = jnp.exp2((s - wide_top) * scale2)
            total = fold(total, p, jnp.add)
            mixed += dot_nn(p.astype(BF16), near(at, 1))
        top4[ry], sum4[ry], mix4[ry] = top, total, mixed

    def forward_mem(i):
        def pair(n, _):
            rys = [n * 2, n * 2 + 1]
            scores = [dot_nt(q4[ry], stored(ry, i, 0)) for ry in rys]
            for ry, s in zip(rys, scores):
                if i * PER < R - SURE:
                    parts = []
                    for b in range(PER):
                        dead = (tab[ry, i * PER + b] >> 8).astype(F32)
                        parts.append(s[:, b * BLOCK : (b + 1) * BLOCK] + dead * NEG)
                    s = jnp.concatenate(parts, axis=1)
                old = top4[ry]
                top = jnp.max(fold(s[:, :DH], s[:, DH:], jnp.maximum), axis=1, keepdims=True)
                top = jnp.maximum(old, jnp.broadcast_to(top, (SEG, DH)))
                less = jnp.exp2((old - top) * scale2)
                p = jnp.exp2((s - jnp.concatenate([top] * (WIDE // DH), axis=1)) * scale2)
                sum4[ry] = fold(sum4[ry] * less, p, jnp.add)
                p = p.astype(BF16)
                p_mem[ry, i] = p
                mix4[ry] = mix4[ry] * less + dot_nn(p, stored(ry, i, 1))
                top4[ry] = top
                m_mem[ry, i] = top
            return _

        lax.fori_loop(0, NY // 2, pair, 0)

    def finish(ry):
        inv = 1.0 / jnp.sum(sum4[ry], axis=1, keepdims=True)
        attn = (mix4[ry] * inv).astype(BF16)
        attn4[ry] = attn
        delta = jnp.sum(do4[ry].astype(F32) * attn.astype(F32), axis=1, keepdims=True)
        stat[ry, 0] = top4[ry]
        stat[ry, 1] = jnp.broadcast_to(inv, (SEG, DH))
        stat[ry, 2] = jnp.broadcast_to(delta, (SEG, DH))

    half = SEG // 2
    for ry in order:
        z_part(0, ry)
    for d in (1, 3, 2):
        send(q_ref.at[:, cols(y_of[d])], q4.at[NY - d], ys.at[d - 1, 2], yr.at[NY - d - 1, 2], y_peer[d])
    lower, upper = pl.ds(0, half), pl.ds(half, half)
    arrived(fg.at[x_of[NX - 1]], xs.at[0], xr.at[0])
    send(fg.at[x_of[NX - 1], lower], fg.at[x_of[NX - 1], lower], xs.at[2], xr.at[2], x_peer[1])
    arrived(fg.at[x_of[1]], xs.at[1], xr.at[1])
    send(fg.at[x_of[1], upper], fg.at[x_of[1], upper], xs.at[3], xr.at[3], x_peer[NX - 1])
    for ry in range(NY):
        make_table(ry)
    to_smem = pltpu.make_async_copy(tab_v, tab, loc.at[0])
    to_smem.start()
    for ry in order:
        z_part(1, ry)

    arrived(fg.at[x_of[2], lower], xs.at[2], xr.at[2])
    arrived(fg.at[x_of[2], upper], xs.at[3], xr.at[3])
    width = g_ref.shape[1]
    da = dot_nt(fg[0], w_ref[:, :width])
    for i in range(1, NX):
        da += dot_nt(fg[i], w_ref[:, i * width : (i + 1) * width])
    da = da.astype(BF16)
    for i in range(NY):
        dal[i] = da[:, i * DH : (i + 1) * DH]
    do4[0] = dal[y]
    for d in (1, 3, 2):
        send(dal.at[y_of[d]], do4.at[NY - d], ds_.at[d - 1], dr.at[NY - d - 1], y_peer[d])
    for i in range(NX):
        fgt[i] = fg[i].T
    to_smem.wait()
    for ry in range(1, NY):
        arrived(q4.at[ry], ys.at[ry - 1, 2], yr.at[ry - 1, 2])
    for ry in order:
        take(0, ry)
    for ry in order:
        take(NZ - 1, ry)

    def near_step(ry, _):
        forward_near(ry)
        return _

    lax.fori_loop(0, NY, near_step, 0)
    for ry in order:
        z_part(2, ry)
    for rz in (1, NZ - 2, 2):
        for ry in order:
            take(rz, ry)
    forward_mem(0)
    forward_mem(1)
    for n, ry in enumerate(order):
        z_part(3, ry)
        take(NZ - 3, ry)
        take(3, ry)
        forward_mem(2 + n)
    for n in range(2):
        for ry in order[2 * n : 2 * n + 2]:
            z_far(ry)
        for ry in order[2 * n : 2 * n + 2]:
            take(NZ // 2, ry)
        forward_mem(6 + n)
    for ry in range(1, NY):
        arrived(do4.at[ry], ds_.at[ry - 1], dr.at[ry - 1])

    def backward_near(ry):
        q, do = q4[ry], do4[ry]
        top, inv, delta = stat[ry, 0, :, :1], stat[ry, 1, :, :1], stat[ry, 2, :, :1]
        dq = jnp.zeros((SEG, DH), F32)
        for part, at in ((0, ry), (1, cache_slot(ry))):
            weights = jnp.exp2((s_near[ry, part] - top) * scale2) * inv
            slopes = (weights * (dot_nt(do, near(at, 1)) - delta)).astype(BF16)
            dq += dot_nn(slopes, near(at, 0))
            gk_part = dot_tn(slopes, q) * scale
            gv_part = dot_tn(weights.astype(BF16), do)
            if part == 0:
                near_acc[ry, 0] = gk_part
                near_acc[ry, 1] = gv_part
            else:
                carry_out[ry, 0] = gk_part.astype(BF16)
                carry_out[ry, 1] = gv_part.astype(BF16)
        dq_acc[ry] = dq

    def backward_mem(ry):
        do = do4[ry]
        top, inv, delta = stat[ry, 0], stat[ry, 1], stat[ry, 2]
        wide_delta = jnp.concatenate([delta] * (WIDE // DH), axis=1)

        def step(n, dq):
            for i in (2 * n, 2 * n + 1):
                slopes = (p_mem[ry, i].astype(F32) * (dot_nt(do, stored(ry, i, 1)) - wide_delta)).astype(BF16)
                dq += dot_nn(slopes, stored(ry, i, 0)) * jnp.exp2((m_mem[ry, i] - top) * scale2)
            return dq

        dq = lax.fori_loop(0, CHUNKS // 2, step, jnp.zeros((SEG, DH), F32))
        gq[ry] = ((dq_acc[ry] + dq * inv) * scale).astype(BF16)

    for ry in (2, 1, 3, 0):
        finish(ry)
        if ry:
            send(attn4.at[ry], attn_in.at[y], as_.at[ry - 1], ar.at[ry - 1], y_peer[ry])
    attn_in[y] = attn4[0]

    for ry in range(NY):
        backward_near(ry)
        to = lax.rem(ry + NY - wrap, NY)
        send(carry_out.at[ry], carry_in.at[to], cs.at[ry], cr.at[to], back)

    one, two, three = y + 1 - 2 * lax.rem(y, 2), y_of[2], NY - 1 - y
    y_one, y_three = (seg_of(one, z, c), x), (seg_of(three, z, c), x)
    for d in range(1, NY):
        arrived(attn_in.at[y_of[NY - d]], as_.at[d - 1], ar.at[d - 1])
    attn = jnp.concatenate([attn_in[i] for i in range(NY)], axis=1)
    wide = attn.shape[1]
    rows = pg_ref.shape[0]
    for i in range(NY):
        part = dot_nn(fgt[i], attn).reshape(NZ, NC, rows, wide)
        pp[i] = part.astype(BF16)
        send(pp.at[i, :, 1 - c], rs0.at[i], bs.at[i], br.at[i], sibling)
    for i in range(NX):
        lo_out[i] = dot_nn(attn, w_ref[:, i * width : (i + 1) * width]).astype(BF16)
    for d in (1, 3, 2):
        send(lo_out.at[x_of[d]], lo_in.at[d - 1], ls.at[d - 1], lr.at[d - 1], x_peer[d])
    for i in range(NY):
        arrived(rs0.at[i], bs.at[i], br.at[i])
        r1[i] = (pp[i, :, c].astype(F32) + rs0[i].astype(F32)).astype(BF16)
    part_a, part_b = pl.ds(0, NZ // 2), pl.ds(NZ // 2, NZ // 2)
    send(r1.at[two, part_a], ra.at[1], rys.at[0], ryr.at[0], y_one)
    send(r1.at[two, part_b], rb.at[1], rys.at[1], ryr.at[1], y_three)
    send(r1.at[one, part_a], ra.at[0], rys.at[2], ryr.at[2], y_one)
    send(r1.at[three, part_b], rb.at[0], rys.at[3], ryr.at[3], y_three)
    backward_mem(2)
    send(gq.at[2], dq_ref.at[:, cols(y)], os_.at[0, 1], or_.at[0, 1], y_peer[2])
    arrived(ra.at[1], rys.at[0], ryr.at[0])
    ra_out[...] = (r1[three, : NZ // 2].astype(F32) + ra[1].astype(F32)).astype(BF16)
    send(ra_out, ra2, rys.at[4], ryr.at[4], y_three)
    arrived(rb.at[1], rys.at[1], ryr.at[1])
    rb_out[...] = (r1[one, NZ // 2 :].astype(F32) + rb[1].astype(F32)).astype(BF16)
    send(rb_out, rb2, rys.at[5], ryr.at[5], y_one)
    for ry in (2, 1, 3, 0):
        arrived(carry_in.at[ry], cs.at[ry], cr.at[ry])
        gk[ry] = (near_acc[ry, 0] + carry_in[ry, 0].astype(F32)).astype(BF16)
        gv[ry] = (near_acc[ry, 1] + carry_in[ry, 1].astype(F32)).astype(BF16)
        if ry:
            send(gk.at[ry], dk_ref.at[:, cols(y)], os_.at[1, ry - 1], or_.at[1, ry - 1], y_peer[ry])
            send(gv.at[ry], dv_ref.at[:, cols(y)], os_.at[2, ry - 1], or_.at[2, ry - 1], y_peer[ry])
    backward_mem(1)
    send(gq.at[1], dq_ref.at[:, cols(y)], os_.at[0, 0], or_.at[0, 0], y_peer[1])
    arrived(ra.at[0], rys.at[2], ryr.at[2])
    arrived(rb.at[0], rys.at[3], ryr.at[3])
    arrived(ra2, rys.at[4], ryr.at[4])
    r2[: NZ // 2] = (r1[y, : NZ // 2].astype(F32) + ra[0].astype(F32) + ra2[...].astype(F32)).astype(BF16)
    arrived(rb2, rys.at[5], ryr.at[5])
    r2[NZ // 2 :] = (r1[y, NZ // 2 :].astype(F32) + rb[0].astype(F32) + rb2[...].astype(F32)).astype(BF16)
    for d in (4, 3, 5, 2, 6, 1, 7):
        send(r2.at[z_of[d]], rs2.at[d - 1], rzs.at[d - 1], rzr.at[d - 1], z_peer[d])
    backward_mem(3)
    send(gq.at[3], dq_ref.at[:, cols(y)], os_.at[0, 2], or_.at[0, 2], y_peer[3])
    backward_mem(0)

    home = [
        pltpu.make_async_copy(gq.at[0], dq_ref.at[:, cols(y)], loc.at[0]),
        pltpu.make_async_copy(gk.at[0], dk_ref.at[:, cols(y)], loc.at[1]),
        pltpu.make_async_copy(gv.at[0], dv_ref.at[:, cols(y)], loc.at[2]),
    ]
    for copy in home:
        copy.start()
    out = lo_out[x].astype(F32)
    for d in range(1, NX):
        arrived(lo_in.at[d - 1], ls.at[d - 1], lr.at[d - 1])
        out += lo_in[d - 1].astype(F32)
    lo_ref[...] = out.astype(BF16)
    total = r2[z].astype(F32)
    for d in range(1, NZ):
        arrived(rs2.at[d - 1], rzs.at[d - 1], rzr.at[d - 1])
        total += rs2[d - 1].astype(F32)
    pg_ref[...] = total
    for n, ref in enumerate((dq_ref, dk_ref, dv_ref)):
        for d in range(1, NY):
            arrived(ref.at[:, cols(y_of[NY - d])], os_.at[n, d - 1], or_.at[n, d - 1])
    for copy in home:
        copy.wait()
    for copy in sends:
        copy.wait_send()


def hand_over(*refs):
    for i in range(5):
        refs[5 + i][...] = refs[i][...]


def per_device(queries, keys, values, out_grad, out_weight, retr_owner, retr_block):
    tok, wide = queries.shape
    full = out_weight.shape[1]
    rows = full // (NY * NZ * NC)
    vmem = pl.BlockSpec(memory_space=pltpu.VMEM)
    dma = pltpu.SemaphoreType.DMA
    tile = (tok, DH)
    halves = tok // BLOCK
    quarter = (NZ // 2, rows, wide)
    scratch = [
        pltpu.VMEM((NC * NZ * NY, 2, halves, BLOCK, DH), BF16),
        pltpu.VMEM((NC * NZ * NY, 2, halves, BLOCK, DH), BF16),
        pltpu.VMEM((NY,) + tile, BF16),
        pltpu.VMEM((NY,) + tile, BF16),
        pltpu.VMEM((NY,) + tile, BF16),
        pltpu.VMEM((NX, tok, wide), BF16),
        pltpu.VMEM((NX, wide, tok), BF16),
        pltpu.VMEM((NY, 2, tok, tok), F32),
        pltpu.VMEM((NY, CHUNKS, tok, WIDE), BF16),
        pltpu.VMEM((NY, CHUNKS) + tile, F32),
        pltpu.VMEM((NY,) + tile, F32),
        pltpu.VMEM((NY,) + tile, F32),
        pltpu.VMEM((NY,) + tile, F32),
        pltpu.VMEM((NY, 3) + tile, F32),
        pltpu.VMEM((NY,) + tile, BF16),
        pltpu.VMEM((NY,) + tile, BF16),
        pltpu.VMEM((NX, tok, wide), BF16),
        pltpu.VMEM((NX - 1, tok, wide), BF16),
        pltpu.VMEM((NY, NZ, NC, rows, wide), BF16),
        pltpu.VMEM((NY, NZ, rows, wide), BF16),
        pltpu.VMEM((NY, NZ, rows, wide), BF16),
        pltpu.VMEM((2,) + quarter, BF16),
        pltpu.VMEM((2,) + quarter, BF16),
        pltpu.VMEM(quarter, BF16),
        pltpu.VMEM(quarter, BF16),
        pltpu.VMEM(quarter, BF16),
        pltpu.VMEM(quarter, BF16),
        pltpu.VMEM((NZ, rows, wide), BF16),
        pltpu.VMEM((NZ - 1, rows, wide), BF16),
        pltpu.VMEM((NY,) + tile, F32),
        pltpu.VMEM((NY, 2) + tile, F32),
        pltpu.VMEM((NY, 2) + tile, BF16),
        pltpu.VMEM((NY, 2) + tile, BF16),
        pltpu.VMEM((NY,) + tile, BF16),
        pltpu.VMEM((NY,) + tile, BF16),
        pltpu.VMEM((NY,) + tile, BF16),
        pltpu.VMEM((8, DH), jnp.int32),
        pltpu.SMEM((8, DH), jnp.int32),
        dma((4,)),
        dma((NY - 1, 3)), dma((NY - 1, 3)),
        dma((4,)), dma((4,)),
        dma((2, NZ // 2, NY)), dma((2, NZ // 2, NY)),
        dma((NZ, NY)), dma((NZ, NY)),
        dma((NY - 1,)), dma((NY - 1,)),
        dma((NY - 1,)), dma((NY - 1,)),
        dma((NY,)), dma((NY,)),
        dma((NY,)), dma((NY,)),
        dma((6,)), dma((6,)),
        dma((NZ - 1,)), dma((NZ - 1,)),
        dma((NX - 1,)), dma((NX - 1,)),
        dma((3, NY - 1)), dma((3, NY - 1)),
    ]
    grad = jax.ShapeDtypeStruct((tok, wide), BF16)
    shapes = (grad, grad, grad, grad, jax.ShapeDtypeStruct((rows, wide), F32))
    results = pl.pallas_call(
        kernel,
        out_shape=shapes,
        in_specs=[vmem] * 7,
        out_specs=(vmem,) * 5,
        scratch_shapes=scratch,
        compiler_params=pltpu.CompilerParams(
            collective_id=0, has_side_effects=True, vmem_limit_bytes=60 * 1024 * 1024
        ),
    )(
        retr_owner.T,
        retr_block.T,
        queries,
        keys.reshape(halves, BLOCK, wide),
        values.reshape(halves, BLOCK, wide),
        out_grad,
        out_weight,
    )
    return pl.pallas_call(hand_over, out_shape=shapes, in_specs=[vmem] * 5, out_specs=(vmem,) * 5)(*results)


def solution(mesh):
    rows = P("seg", "head")
    return jax.shard_map(
        per_device,
        mesh=mesh,
        in_specs=(rows, rows, rows, rows, P("head", None), P(), P()),
        out_specs=(rows,) * 5,
        check_vma=False,
    )
```

```python
import math

import jax
import jax.numpy as jnp
from jax import lax
from jax.experimental import pallas as pl
from jax.experimental.pallas import tpu as pltpu
from jax.sharding import PartitionSpec as P

DH = 128
BLOCK = 128
SEG = 256
R = 32
NY, NZ, NC, NX = 4, 8, 2, 4
MESH = pl.DeviceIdType.MESH
F32, BF16 = jnp.float32, jnp.bfloat16
NEG = -1e30
SURE = 24
PER = 4
WIDE = PER * BLOCK
CHUNKS = R // PER


def dot_nt(a, b):
    return lax.dot_general(a, b, (((1,), (1,)), ((), ())), preferred_element_type=F32)


def dot_nn(a, b):
    return lax.dot_general(a, b, (((1,), (0,)), ((), ())), preferred_element_type=F32)


def dot_tn(a, b):
    return lax.dot_general(a, b, (((0,), (0,)), ((), ())), preferred_element_type=F32)


def kernel(
    owner_ref, block_ref, q_ref, k_ref, v_ref, g_ref, w_ref,
    lo_ref, dq_ref, dk_ref, dv_ref, pg_ref,
    w_v, lo_v, kv, kvc, q4, do4, g4, s_near, p_mem, m_mem, top4, sum4, mix4, stat, attn4, attn_in, lo_out, lo_in,
    pt, pp, rs0, r1, rs2, r2, dq_acc, near_acc, carry_out, carry_in, gq, gk, gv, tab_v, tab,
    loc, ys, yr, gs, gr, xs, xr, zs, zr, ms, mr, as_, ar, bs, br, cs, cr, rzs, rzr, ls, lr, ps, pr, os_, or_,
):
    s_me = lax.axis_index("seg")
    x = lax.axis_index("head")
    c = lax.rem(s_me, NC)
    z = lax.rem(lax.div(s_me, NC), NZ)
    y = lax.div(s_me, NC * NZ)
    scale = 1.0 / math.sqrt(DH)
    scale2 = scale * math.log2(math.e)

    def seg_of(yy, zz, cc):
        return (yy * NZ + zz) * NC + cc

    y_of = [lax.rem(y + d, NY) for d in range(NY)]
    x_of = [lax.rem(x + d, NX) for d in range(NX)]
    z_of = [lax.rem(z + d, NZ) for d in range(NZ)]
    y_peer = [(seg_of(y_of[d], z, c), x) for d in range(NY)]
    z_peer = [(seg_of(y, z_of[d], c), x) for d in range(NZ)]
    x_peer = [(s_me, x_of[d]) for d in range(NX)]
    sibling = (seg_of(y, z, 1 - c), x)
    cross = (seg_of(y, lax.rem(z + NZ - 1 + 2 * c, NZ), 1 - c), x)
    back = (seg_of(y, lax.rem(z + NZ - 1 + c, NZ), 1 - c), x)
    wrap = 1 - jnp.minimum(z + c, 1)

    sends = []

    def send(src, dst, ssem, rsem, dev):
        copy = pltpu.make_async_remote_copy(
            src_ref=src, dst_ref=dst, send_sem=ssem, recv_sem=rsem, device_id=dev, device_id_type=MESH
        )
        copy.start()
        sends.append(copy)

    def arrived(dst, ssem, rsem):
        pltpu.make_async_remote_copy(
            src_ref=dst, dst_ref=dst, send_sem=ssem, recv_sem=rsem, device_id=sibling, device_id_type=MESH
        ).wait_recv()

    def cols(i):
        return pl.ds(pl.multiple_of(i * DH, DH), DH)

    def slot(plane, rz, ry):
        return (plane * NZ + rz) * NY + ry

    own = [
        pltpu.make_async_copy(k_ref.at[:, :, cols(y)], kv.at[0, 0], loc.at[0]),
        pltpu.make_async_copy(v_ref.at[:, :, cols(y)], kv.at[0, 1], loc.at[1]),
        pltpu.make_async_copy(q_ref.at[:, cols(y)], q4.at[0], loc.at[2]),
        pltpu.make_async_copy(g_ref, g4.at[0, x], loc.at[3]),
    ]
    weights_in = pltpu.make_async_copy(w_ref, w_v, loc.at[4])
    for copy in own + [weights_in]:
        copy.start()

    barrier = pltpu.get_barrier_semaphore()
    peers = y_peer[1:] + z_peer[1:] + x_peer[1:] + [sibling, cross]
    for dev in peers:
        pl.semaphore_signal(barrier, inc=1, device_id=dev, device_id_type=MESH)
    pl.semaphore_wait(barrier, len(peers))

    for d in (1, 3, 2):
        send(k_ref.at[:, :, cols(y_of[d])], kv.at[NY - d, 0], ys.at[d - 1, 0], yr.at[NY - d - 1, 0], y_peer[d])
        send(v_ref.at[:, :, cols(y_of[d])], kv.at[NY - d, 1], ys.at[d - 1, 1], yr.at[NY - d - 1, 1], y_peer[d])
    send(g_ref, g4.at[0, x], xs.at[0, 0], xr.at[0, 0], x_peer[1])
    send(g_ref, g4.at[0, x], xs.at[0, 1], xr.at[0, 1], x_peer[NX - 1])
    for copy in own:
        copy.wait()
    order = (0, 1, 3, 2)

    def z_part(t, ry):
        up, down = (NZ - t) % NZ, t
        if t == 0:
            if ry:
                arrived(kv.at[ry, 0], ys.at[ry - 1, 0], yr.at[ry - 1, 0])
                arrived(kv.at[ry, 1], ys.at[ry - 1, 1], yr.at[ry - 1, 1])
        else:
            arrived(kv.at[slot(0, up, ry)], zs.at[0, t - 1, ry], zr.at[0, t - 1, ry])
            arrived(kv.at[slot(0, down, ry)], zs.at[1, t - 1, ry], zr.at[1, t - 1, ry])
        if t < NZ // 2 - 1:
            send(kv.at[slot(0, up, ry)], kv.at[slot(0, NZ - 1 - t, ry)], zs.at[0, t, ry], zr.at[0, t, ry], z_peer[1])
            send(kv.at[slot(0, down, ry)], kv.at[slot(0, t + 1, ry)], zs.at[1, t, ry], zr.at[1, t, ry], z_peer[NZ - 1])
        else:
            far = slot(0, NZ // 2, ry)
            send(kv.at[slot(0, up, ry), 0], kv.at[far, 0], zs.at[0, t, ry], zr.at[0, t, ry], z_peer[1])
            send(kv.at[slot(0, down, ry), 1], kv.at[far, 1], zs.at[1, t, ry], zr.at[1, t, ry], z_peer[NZ - 1])
        for rz in ((0,) if t == 0 else (up, down)):
            send(kv.at[slot(0, rz, ry)], kv.at[slot(1, rz, ry)], ms.at[rz, ry], mr.at[rz, ry], sibling)

    def z_far(ry):
        far, t = slot(0, NZ // 2, ry), NZ // 2 - 1
        arrived(kv.at[far, 0], zs.at[0, t, ry], zr.at[0, t, ry])
        arrived(kv.at[far, 1], zs.at[1, t, ry], zr.at[1, t, ry])
        send(kv.at[far], kv.at[slot(1, NZ // 2, ry)], ms.at[NZ // 2, ry], mr.at[NZ // 2, ry], sibling)

    def take(rz, ry):
        arrived(kv.at[slot(1, rz, ry)], ms.at[rz, ry], mr.at[rz, ry])
        for plane in range(NC):
            kvc[slot(plane, rz, ry)] = kv[slot(plane, rz, ry)]

    def seg_id(ry):
        return seg_of(lax.rem(y + ry, NY), z, c)

    def cache_slot(ry):
        return slot(1, (NZ - 1) * (1 - c), lax.rem(ry + NY - wrap, NY))

    def near(at, which):
        return kvc[at, which].reshape(SEG, DH)

    def fold(m, entry, op):
        for i in range(entry.shape[1] // DH):
            m = op(m, entry[:, i * DH : (i + 1) * DH])
        return m

    def make_table(ry):
        lane = lax.broadcasted_iota(jnp.int32, owner_ref.shape, 1) == seg_id(ry)
        o = jnp.sum(jnp.where(lane, owner_ref[...], 0), axis=1, keepdims=True)
        b = jnp.sum(jnp.where(lane, block_ref[...], 0), axis=1, keepdims=True)
        rz = ((o >> 1) & (NZ - 1)) + NZ - z & (NZ - 1)
        rr = (o >> 4) + NY - y & (NY - 1)
        plane = (o + c) & (NC - 1)
        away = jnp.minimum(rz, NZ - rz)
        dead = b < 0
        turn = rr ^ (rr >> 1)
        stage = jnp.where(away < 3, 0, jnp.where(away == 3, 1 + turn, 1 + NY + turn))
        stage = jnp.where(dead, -1, stage)
        code = jnp.where(dead, 256, ((plane * NZ + rz) * NY + rr) * 2 + jnp.maximum(b, 0))
        down = lax.broadcasted_iota(jnp.int32, (R, R), 0)
        across = lax.broadcasted_iota(jnp.int32, (R, R), 1)
        stage_col = jnp.broadcast_to(stage, (R, R))
        stage_row = jnp.sum(jnp.where(down == across, stage_col, 0), axis=0, keepdims=True)
        first = (stage_row < stage_col) | ((stage_row == stage_col) & (across < down))
        rank = jnp.sum(first.astype(jnp.int32), axis=1, keepdims=True)
        tab_v[ry : ry + 1, :R] = jnp.sum(jnp.where(rank == across, code, 0), axis=0, keepdims=True)

    def stored(ry, i, which):
        parts = []
        for b in range(PER):
            code = tab[ry, i * PER + b]
            parts.append(kvc[(code & 255) >> 1, which, code & 1])
        return jnp.concatenate(parts, axis=0)

    causal = lax.broadcasted_iota(jnp.int32, (SEG, SEG), 0) >= lax.broadcasted_iota(jnp.int32, (SEG, SEG), 1)

    def forward_near(ry):
        q = q4[ry]
        s_own = jnp.where(causal, dot_nt(q, near(ry, 0)), NEG)
        s_near[ry, 0] = s_own
        dead = (1 - jnp.minimum(seg_id(ry), 1)).astype(F32)
        s_cache = dot_nt(q, near(cache_slot(ry), 0)) + dead * NEG
        s_near[ry, 1] = s_cache
        top = fold(fold(s_own[:, :DH], s_own[:, DH:], jnp.maximum), s_cache, jnp.maximum)
        top = jnp.broadcast_to(jnp.max(top, axis=1, keepdims=True), (SEG, DH))
        total = jnp.zeros((SEG, DH), F32)
        mixed = jnp.zeros((SEG, DH), F32)
        wide_top = jnp.concatenate([top] * (SEG // DH), axis=1)
        for s, at in ((s_own, ry), (s_cache, cache_slot(ry))):
            p = jnp.exp2((s - wide_top) * scale2)
            total = fold(total, p, jnp.add)
            mixed += dot_nn(p.astype(BF16), near(at, 1))
        top4[ry], sum4[ry], mix4[ry] = top, total, mixed

    def forward_mem(i):
        def pair(n, _):
            rys = [n * 2, n * 2 + 1]
            scores = [dot_nt(q4[ry], stored(ry, i, 0)) for ry in rys]
            for ry, s in zip(rys, scores):
                if i * PER < R - SURE:
                    parts = []
                    for b in range(PER):
                        dead = (tab[ry, i * PER + b] >> 8).astype(F32)
                        parts.append(s[:, b * BLOCK : (b + 1) * BLOCK] + dead * NEG)
                    s = jnp.concatenate(parts, axis=1)
                old = top4[ry]
                top = jnp.max(fold(s[:, :DH], s[:, DH:], jnp.maximum), axis=1, keepdims=True)
                top = jnp.maximum(old, jnp.broadcast_to(top, (SEG, DH)))
                less = jnp.exp2((old - top) * scale2)
                p = jnp.exp2((s - jnp.concatenate([top] * (WIDE // DH), axis=1)) * scale2)
                sum4[ry] = fold(sum4[ry] * less, p, jnp.add)
                p = p.astype(BF16)
                p_mem[ry, i] = p
                mix4[ry] = mix4[ry] * less + dot_nn(p, stored(ry, i, 1))
                top4[ry] = top
                m_mem[ry, i] = top
            return _

        lax.fori_loop(0, NY // 2, pair, 0)

    def finish(ry):
        inv = 1.0 / jnp.sum(sum4[ry], axis=1, keepdims=True)
        attn = (mix4[ry] * inv).astype(BF16)
        attn4[ry] = attn
        delta = jnp.sum(do4[ry].astype(F32) * attn.astype(F32), axis=1, keepdims=True)
        stat[ry, 0] = top4[ry]
        stat[ry, 1] = jnp.broadcast_to(inv, (SEG, DH))
        stat[ry, 2] = jnp.broadcast_to(delta, (SEG, DH))

    lower, upper = pl.ds(0, SEG // 2), pl.ds(SEG // 2, SEG // 2)
    width = g4.shape[3]

    def x_first(ry):
        arrived(g4.at[ry, x], gs.at[ry - 1], gr.at[ry - 1])
        send(g4.at[ry, x], g4.at[ry, x], xs.at[ry, 0], xr.at[ry, 0], x_peer[1])
        send(g4.at[ry, x], g4.at[ry, x], xs.at[ry, 1], xr.at[ry, 1], x_peer[NX - 1])

    def x_second(ry):
        left, right = x_of[NX - 1], x_of[1]
        arrived(g4.at[ry, left], xs.at[ry, 0], xr.at[ry, 0])
        send(g4.at[ry, left, lower], g4.at[ry, left, lower], xs.at[ry, 2], xr.at[ry, 2], x_peer[1])
        arrived(g4.at[ry, right], xs.at[ry, 1], xr.at[ry, 1])
        send(g4.at[ry, right, upper], g4.at[ry, right, upper], xs.at[ry, 3], xr.at[ry, 3], x_peer[NX - 1])

    def d_attn(ry):
        arrived(g4.at[ry, x_of[2], lower], xs.at[ry, 2], xr.at[ry, 2])
        arrived(g4.at[ry, x_of[2], upper], xs.at[ry, 3], xr.at[ry, 3])
        da = jnp.zeros((SEG, DH), F32)
        for i in range(NX):
            da += dot_nt(g4[ry, i], w_v[cols(y), i * width : (i + 1) * width])
        do4[ry] = da.astype(BF16)

    def g_send(d):
        send(g_ref, g4.at[NY - d, x], gs.at[d - 1], gr.at[NY - d - 1], y_peer[d])

    z_part(0, order[0])
    z_part(0, order[1])
    g_send(3)
    z_part(0, order[2])
    g_send(1)
    g_send(2)
    for d in (1, 3, 2):
        send(q_ref.at[:, cols(y_of[d])], q4.at[NY - d], ys.at[d - 1, 2], yr.at[NY - d - 1, 2], y_peer[d])
    z_part(0, order[3])
    for ry in range(NY):
        make_table(ry)
    to_smem = pltpu.make_async_copy(tab_v, tab, loc.at[0])
    to_smem.start()
    z_part(1, order[0])
    x_second(0)
    z_part(1, order[1])
    x_first(1)
    z_part(1, order[2])
    x_first(3)
    z_part(1, order[3])
    x_first(2)
    weights_in.wait()
    d_attn(0)
    to_smem.wait()
    for ry in range(1, NY):
        arrived(q4.at[ry], ys.at[ry - 1, 2], yr.at[ry - 1, 2])
    for ry in order:
        take(0, ry)
    for ry in order:
        take(NZ - 1, ry)

    def near_step(ry, _):
        forward_near(ry)
        return _

    lax.fori_loop(0, NY, near_step, 0)
    z_part(2, order[0])
    z_part(2, order[1])
    x_second(1)
    z_part(2, order[2])
    z_part(2, order[3])
    for rz in (1, NZ - 2, 2):
        for ry in order:
            take(rz, ry)
    x_second(3)
    forward_mem(0)
    forward_mem(1)
    for n, ry in enumerate(order):
        z_part(3, ry)
        take(NZ - 3, ry)
        take(3, ry)
        if n == 0:
            x_second(2)
        forward_mem(2 + n)
        if n == 0:
            d_attn(1)
        if n == 1:
            d_attn(3)
    for n in range(2):
        for ry in order[2 * n : 2 * n + 2]:
            z_far(ry)
        for ry in order[2 * n : 2 * n + 2]:
            take(NZ // 2, ry)
        forward_mem(6 + n)
        if n == 0:
            d_attn(2)

    def backward_near(ry):
        q, do = q4[ry], do4[ry]
        top, inv, delta = stat[ry, 0, :, :1], stat[ry, 1, :, :1], stat[ry, 2, :, :1]
        dq = jnp.zeros((SEG, DH), F32)
        for part, at in ((0, ry), (1, cache_slot(ry))):
            weights = jnp.exp2((s_near[ry, part] - top) * scale2) * inv
            slopes = (weights * (dot_nt(do, near(at, 1)) - delta)).astype(BF16)
            dq += dot_nn(slopes, near(at, 0))
            gk_part = dot_tn(slopes, q) * scale
            gv_part = dot_tn(weights.astype(BF16), do)
            if part == 0:
                near_acc[ry, 0] = gk_part
                near_acc[ry, 1] = gv_part
            else:
                carry_out[ry, 0] = gk_part.astype(BF16)
                carry_out[ry, 1] = gv_part.astype(BF16)
        dq_acc[ry] = dq

    def backward_mem(ry):
        do = do4[ry]
        top, inv, delta = stat[ry, 0], stat[ry, 1], stat[ry, 2]
        wide_delta = jnp.concatenate([delta] * (WIDE // DH), axis=1)

        def step(n, dq):
            for i in [4 * n + k for k in range(4)]:
                slopes = (p_mem[ry, i].astype(F32) * (dot_nt(do, stored(ry, i, 1)) - wide_delta)).astype(BF16)
                dq += dot_nn(slopes, stored(ry, i, 0)) * jnp.exp2((m_mem[ry, i] - top) * scale2)
            return dq

        dq = lax.fori_loop(0, CHUNKS // 4, step, jnp.zeros((SEG, DH), F32))
        gq[ry] = ((dq_acc[ry] + dq * inv) * scale).astype(BF16)

    for n, ry in enumerate((2, 1, 3, 0)):
        finish(ry)
        if ry:
            send(attn4.at[ry], attn_in.at[y], as_.at[ry - 1], ar.at[ry - 1], y_peer[ry])
        turned = attn4[ry].T
        for i in range(NX):
            part = dot_nn(turned, g4[ry, i])
            pt[i] = part if n == 0 else pt[i] + part
    attn_in[y] = attn4[0]

    rows = pg_ref.shape[0]
    for i in range(NY):
        pp[i] = pt[i].T.astype(BF16).reshape(NZ, NC, rows, DH)
        send(pp.at[i, :, 1 - c], rs0.at[i], bs.at[i], br.at[i], sibling)
    for ry in range(NY):
        backward_near(ry)
        to = lax.rem(ry + NY - wrap, NY)
        send(carry_out.at[ry], carry_in.at[to], cs.at[ry], cr.at[to], back)
    for i in range(NY):
        arrived(rs0.at[i], bs.at[i], br.at[i])
        r1[:, i] = (pp[i, :, c].astype(F32) + rs0[i].astype(F32)).astype(BF16)
    for d in (4, 3, 5, 2, 6, 1, 7):
        send(r1.at[z_of[d]], rs2.at[d - 1], rzs.at[d - 1], rzr.at[d - 1], z_peer[d])

    for d in (1, 3, 2):
        arrived(attn_in.at[y_of[NY - d]], as_.at[d - 1], ar.at[d - 1])
    attn = jnp.concatenate([attn_in[i] for i in range(NY)], axis=1)
    for i in range(NX):
        lo_out[i] = dot_nn(attn, w_v[:, i * width : (i + 1) * width]).astype(BF16)
    for d in (2, 1, 3):
        send(lo_out.at[x_of[d]], lo_in.at[d - 1], ls.at[d - 1], lr.at[d - 1], x_peer[d])
    backward_mem(2)
    send(gq.at[2], dq_ref.at[:, cols(y)], os_.at[0, 1], or_.at[0, 1], y_peer[2])
    for ry in (2, 1, 3, 0):
        arrived(carry_in.at[ry], cs.at[ry], cr.at[ry])
        gk[ry] = (near_acc[ry, 0] + carry_in[ry, 0].astype(F32)).astype(BF16)
        gv[ry] = (near_acc[ry, 1] + carry_in[ry, 1].astype(F32)).astype(BF16)
        if ry:
            send(gk.at[ry], dk_ref.at[:, cols(y)], os_.at[1, ry - 1], or_.at[1, ry - 1], y_peer[ry])
            send(gv.at[ry], dv_ref.at[:, cols(y)], os_.at[2, ry - 1], or_.at[2, ry - 1], y_peer[ry])
    backward_mem(1)
    send(gq.at[1], dq_ref.at[:, cols(y)], os_.at[0, 0], or_.at[0, 0], y_peer[1])
    total = r1[z].astype(F32)
    for d in range(1, NZ):
        arrived(rs2.at[d - 1], rzs.at[d - 1], rzr.at[d - 1])
        total += rs2[d - 1].astype(F32)
    r2[...] = total
    for d in (2, 1, 3):
        send(r2.at[y_of[d]], pg_ref.at[:, cols(y)], ps.at[d - 1], pr.at[d - 1], y_peer[d])
    backward_mem(3)
    send(gq.at[3], dq_ref.at[:, cols(y)], os_.at[0, 2], or_.at[0, 2], y_peer[3])
    backward_mem(0)

    home = [
        pltpu.make_async_copy(gq.at[0], dq_ref.at[:, cols(y)], loc.at[0]),
        pltpu.make_async_copy(gk.at[0], dk_ref.at[:, cols(y)], loc.at[1]),
        pltpu.make_async_copy(gv.at[0], dv_ref.at[:, cols(y)], loc.at[2]),
        pltpu.make_async_copy(r2.at[y], pg_ref.at[:, cols(y)], loc.at[5]),
    ]
    for copy in home:
        copy.start()
    out = lo_out[x].astype(F32)
    for d in range(1, NX):
        arrived(lo_in.at[d - 1], ls.at[d - 1], lr.at[d - 1])
        out += lo_in[d - 1].astype(F32)
    lo_v[...] = out.astype(BF16)
    home.append(pltpu.make_async_copy(lo_v, lo_ref, loc.at[3]))
    home[-1].start()
    for d in range(1, NY):
        arrived(pg_ref.at[:, cols(y_of[NY - d])], ps.at[d - 1], pr.at[d - 1])
    for n, ref in enumerate((dq_ref, dk_ref, dv_ref)):
        for d in range(1, NY):
            arrived(ref.at[:, cols(y_of[NY - d])], os_.at[n, d - 1], or_.at[n, d - 1])
    for copy in home:
        copy.wait()
    for copy in sends:
        copy.wait_send()


def hand_over(*refs):
    for i in range(5):
        refs[5 + i][...] = refs[i][...]


def per_device(queries, keys, values, out_grad, out_weight, retr_owner, retr_block):
    tok, wide = queries.shape
    full = out_weight.shape[1]
    rows = full // (NY * NZ * NC)
    vmem = pl.BlockSpec(memory_space=pltpu.VMEM)
    anywhere = pl.BlockSpec(memory_space=pl.ANY)
    dma = pltpu.SemaphoreType.DMA
    tile = (tok, DH)
    halves = tok // BLOCK
    scratch = [
        pltpu.VMEM((wide, full), BF16),
        pltpu.VMEM((tok, wide), BF16),
        pltpu.VMEM((NC * NZ * NY, 2, halves, BLOCK, DH), BF16),
        pltpu.VMEM((NC * NZ * NY, 2, halves, BLOCK, DH), BF16),
        pltpu.VMEM((NY,) + tile, BF16),
        pltpu.VMEM((NY,) + tile, BF16),
        pltpu.VMEM((NY, NX, tok, wide), BF16),
        pltpu.VMEM((NY, 2, tok, tok), F32),
        pltpu.VMEM((NY, CHUNKS, tok, WIDE), BF16),
        pltpu.VMEM((NY, CHUNKS) + tile, F32),
        pltpu.VMEM((NY,) + tile, F32),
        pltpu.VMEM((NY,) + tile, F32),
        pltpu.VMEM((NY,) + tile, F32),
        pltpu.VMEM((NY, 3) + tile, F32),
        pltpu.VMEM((NY,) + tile, BF16),
        pltpu.VMEM((NY,) + tile, BF16),
        pltpu.VMEM((NX, tok, wide), BF16),
        pltpu.VMEM((NX - 1, tok, wide), BF16),
        pltpu.VMEM((NX, DH, wide), F32),
        pltpu.VMEM((NY, NZ, NC, rows, DH), BF16),
        pltpu.VMEM((NY, NZ, rows, DH), BF16),
        pltpu.VMEM((NZ, NY, rows, DH), BF16),
        pltpu.VMEM((NZ - 1, NY, rows, DH), BF16),
        pltpu.VMEM((NY, rows, DH), F32),
        pltpu.VMEM((NY,) + tile, F32),
        pltpu.VMEM((NY, 2) + tile, F32),
        pltpu.VMEM((NY, 2) + tile, BF16),
        pltpu.VMEM((NY, 2) + tile, BF16),
        pltpu.VMEM((NY,) + tile, BF16),
        pltpu.VMEM((NY,) + tile, BF16),
        pltpu.VMEM((NY,) + tile, BF16),
        pltpu.VMEM((8, DH), jnp.int32),
        pltpu.SMEM((8, DH), jnp.int32),
        dma((6,)),
        dma((NY - 1, 3)), dma((NY - 1, 3)),
        dma((NY - 1,)), dma((NY - 1,)),
        dma((NY, 4)), dma((NY, 4)),
        dma((2, NZ // 2, NY)), dma((2, NZ // 2, NY)),
        dma((NZ, NY)), dma((NZ, NY)),
        dma((NY - 1,)), dma((NY - 1,)),
        dma((NY,)), dma((NY,)),
        dma((NY,)), dma((NY,)),
        dma((NZ - 1,)), dma((NZ - 1,)),
        dma((NX - 1,)), dma((NX - 1,)),
        dma((NY - 1,)), dma((NY - 1,)),
        dma((3, NY - 1)), dma((3, NY - 1)),
    ]
    grad = jax.ShapeDtypeStruct((tok, wide), BF16)
    shapes = (grad, grad, grad, grad, jax.ShapeDtypeStruct((rows, wide), F32))
    results = pl.pallas_call(
        kernel,
        out_shape=shapes,
        in_specs=[vmem] * 2 + [anywhere] * 5,
        out_specs=(anywhere,) * 5,
        scratch_shapes=scratch,
        compiler_params=pltpu.CompilerParams(
            collective_id=0, has_side_effects=True, vmem_limit_bytes=60 * 1024 * 1024
        ),
    )(
        retr_owner.T,
        retr_block.T,
        queries,
        keys.reshape(halves, BLOCK, wide),
        values.reshape(halves, BLOCK, wide),
        out_grad,
        out_weight,
    )
    return pl.pallas_call(hand_over, out_shape=shapes, in_specs=[vmem] * 5, out_specs=(vmem,) * 5)(*results)


def solution(mesh):
    rows = P("seg", "head")
    return jax.shard_map(
        per_device,
        mesh=mesh,
        in_specs=(rows, rows, rows, rows, P("head", None), P(), P()),
        out_specs=(rows,) * 5,
        check_vma=False,
    )
```

```python
import math

import jax
import jax.numpy as jnp
from jax import lax
from jax.experimental import pallas as pl
from jax.experimental.pallas import tpu as pltpu
from jax.sharding import PartitionSpec as P

DH = 128
BLOCK = 128
SEG = 256
R = 32
NY, NZ, NC, NX = 4, 8, 2, 4
MESH = pl.DeviceIdType.MESH
F32, BF16 = jnp.float32, jnp.bfloat16
NEG = -1e30
SURE = 24
PER = 4
WIDE = PER * BLOCK
CHUNKS = R // PER


def dot_nt(a, b):
    return lax.dot_general(a, b, (((1,), (1,)), ((), ())), preferred_element_type=F32)


def dot_nn(a, b):
    return lax.dot_general(a, b, (((1,), (0,)), ((), ())), preferred_element_type=F32)


def dot_tn(a, b):
    return lax.dot_general(a, b, (((0,), (0,)), ((), ())), preferred_element_type=F32)


def kernel(
    owner_ref, block_ref, q_ref, k_ref, v_ref, g_ref, w_ref,
    lo_ref, dq_ref, dk_ref, dv_ref, pg_ref,
    w_v, lo_v, kv, kvc, q4, do4, g4, s_near, p_mem, m_mem, top4, sum4, mix4, stat, attn4, attn_in, lo_out, lo_in,
    pt, pp, rs0, r1, rs2, r2, dq_acc, near_acc, carry_out, carry_in, gq, gk, gv, tab_v, tab,
    loc, ys, yr, gs, gr, xs, xr, zs, zr, ms, mr, as_, ar, bs, br, cs, cr, rzs, rzr, ls, lr, ps, pr, os_, or_,
):
    s_me = lax.axis_index("seg")
    x = lax.axis_index("head")
    c = lax.rem(s_me, NC)
    z = lax.rem(lax.div(s_me, NC), NZ)
    y = lax.div(s_me, NC * NZ)
    scale = 1.0 / math.sqrt(DH)
    scale2 = scale * math.log2(math.e)

    def seg_of(yy, zz, cc):
        return (yy * NZ + zz) * NC + cc

    y_of = [lax.rem(y + d, NY) for d in range(NY)]
    x_of = [lax.rem(x + d, NX) for d in range(NX)]
    z_of = [lax.rem(z + d, NZ) for d in range(NZ)]
    y_peer = [(seg_of(y_of[d], z, c), x) for d in range(NY)]
    z_peer = [(seg_of(y, z_of[d], c), x) for d in range(NZ)]
    x_peer = [(s_me, x_of[d]) for d in range(NX)]
    sibling = (seg_of(y, z, 1 - c), x)
    cross = (seg_of(y, lax.rem(z + NZ - 1 + 2 * c, NZ), 1 - c), x)
    back = (seg_of(y, lax.rem(z + NZ - 1 + c, NZ), 1 - c), x)
    wrap = 1 - jnp.minimum(z + c, 1)

    sends = []

    def send(src, dst, ssem, rsem, dev):
        copy = pltpu.make_async_remote_copy(
            src_ref=src, dst_ref=dst, send_sem=ssem, recv_sem=rsem, device_id=dev, device_id_type=MESH
        )
        copy.start()
        sends.append(copy)

    def arrived(dst, ssem, rsem):
        pltpu.make_async_remote_copy(
            src_ref=dst, dst_ref=dst, send_sem=ssem, recv_sem=rsem, device_id=sibling, device_id_type=MESH
        ).wait_recv()

    def cols(i):
        return pl.ds(pl.multiple_of(i * DH, DH), DH)

    def slot(plane, rz, ry):
        return (plane * NZ + rz) * NY + ry

    own = [
        pltpu.make_async_copy(k_ref.at[:, :, cols(y)], kv.at[0, 0], loc.at[0]),
        pltpu.make_async_copy(v_ref.at[:, :, cols(y)], kv.at[0, 1], loc.at[1]),
        pltpu.make_async_copy(q_ref.at[:, cols(y)], q4.at[0], loc.at[2]),
        pltpu.make_async_copy(g_ref, g4.at[0, x], loc.at[3]),
    ]
    weights_in = pltpu.make_async_copy(w_ref, w_v, loc.at[4])
    for copy in own + [weights_in]:
        copy.start()

    barrier = pltpu.get_barrier_semaphore()
    peers = y_peer[1:] + z_peer[1:] + x_peer[1:] + [sibling, cross]
    for dev in peers:
        pl.semaphore_signal(barrier, inc=1, device_id=dev, device_id_type=MESH)
    pl.semaphore_wait(barrier, len(peers))

    for d in (1, 3, 2):
        send(k_ref.at[:, :, cols(y_of[d])], kv.at[NY - d, 0], ys.at[d - 1, 0], yr.at[NY - d - 1, 0], y_peer[d])
        send(v_ref.at[:, :, cols(y_of[d])], kv.at[NY - d, 1], ys.at[d - 1, 1], yr.at[NY - d - 1, 1], y_peer[d])
    send(g_ref, g4.at[0, x], xs.at[0, 0], xr.at[0, 0], x_peer[1])
    send(g_ref, g4.at[0, x], xs.at[0, 1], xr.at[0, 1], x_peer[NX - 1])
    for copy in own:
        copy.wait()
    order = (0, 1, 3, 2)

    def z_part(t, ry):
        up, down = (NZ - t) % NZ, t
        if t == 0:
            if ry:
                arrived(kv.at[ry, 0], ys.at[ry - 1, 0], yr.at[ry - 1, 0])
                arrived(kv.at[ry, 1], ys.at[ry - 1, 1], yr.at[ry - 1, 1])
        else:
            arrived(kv.at[slot(0, up, ry)], zs.at[0, t - 1, ry], zr.at[0, t - 1, ry])
            arrived(kv.at[slot(0, down, ry)], zs.at[1, t - 1, ry], zr.at[1, t - 1, ry])
        if t < NZ // 2 - 1:
            send(kv.at[slot(0, up, ry)], kv.at[slot(0, NZ - 1 - t, ry)], zs.at[0, t, ry], zr.at[0, t, ry], z_peer[1])
            send(kv.at[slot(0, down, ry)], kv.at[slot(0, t + 1, ry)], zs.at[1, t, ry], zr.at[1, t, ry], z_peer[NZ - 1])
        else:
            far = slot(0, NZ // 2, ry)
            send(kv.at[slot(0, up, ry), 0], kv.at[far, 0], zs.at[0, t, ry], zr.at[0, t, ry], z_peer[1])
            send(kv.at[slot(0, down, ry), 1], kv.at[far, 1], zs.at[1, t, ry], zr.at[1, t, ry], z_peer[NZ - 1])
        for rz in ((0,) if t == 0 else (up, down)):
            send(kv.at[slot(0, rz, ry)], kv.at[slot(1, rz, ry)], ms.at[rz, ry], mr.at[rz, ry], sibling)

    def z_far(ry):
        far, t = slot(0, NZ // 2, ry), NZ // 2 - 1
        arrived(kv.at[far, 0], zs.at[0, t, ry], zr.at[0, t, ry])
        arrived(kv.at[far, 1], zs.at[1, t, ry], zr.at[1, t, ry])
        send(kv.at[far], kv.at[slot(1, NZ // 2, ry)], ms.at[NZ // 2, ry], mr.at[NZ // 2, ry], sibling)

    def take(rz, ry):
        arrived(kv.at[slot(1, rz, ry)], ms.at[rz, ry], mr.at[rz, ry])
        for plane in range(NC):
            kvc[slot(plane, rz, ry)] = kv[slot(plane, rz, ry)]

    def seg_id(ry):
        return seg_of(lax.rem(y + ry, NY), z, c)

    def cache_slot(ry):
        return slot(1, (NZ - 1) * (1 - c), lax.rem(ry + NY - wrap, NY))

    def near(at, which):
        return kvc[at, which].reshape(SEG, DH)

    def fold(m, entry, op):
        for i in range(entry.shape[1] // DH):
            m = op(m, entry[:, i * DH : (i + 1) * DH])
        return m

    def make_table(ry):
        lane = lax.broadcasted_iota(jnp.int32, owner_ref.shape, 1) == seg_id(ry)
        o = jnp.sum(jnp.where(lane, owner_ref[...], 0), axis=1, keepdims=True)
        b = jnp.sum(jnp.where(lane, block_ref[...], 0), axis=1, keepdims=True)
        rz = ((o >> 1) & (NZ - 1)) + NZ - z & (NZ - 1)
        rr = (o >> 4) + NY - y & (NY - 1)
        plane = (o + c) & (NC - 1)
        away = jnp.minimum(rz, NZ - rz)
        dead = b < 0
        turn = rr ^ (rr >> 1)
        stage = jnp.where(away < 3, 0, jnp.where(away == 3, 1 + turn, 1 + NY + turn))
        stage = jnp.where(dead, -1, stage)
        code = jnp.where(dead, 256, ((plane * NZ + rz) * NY + rr) * 2 + jnp.maximum(b, 0))
        down = lax.broadcasted_iota(jnp.int32, (R, R), 0)
        across = lax.broadcasted_iota(jnp.int32, (R, R), 1)
        stage_col = jnp.broadcast_to(stage, (R, R))
        stage_row = jnp.sum(jnp.where(down == across, stage_col, 0), axis=0, keepdims=True)
        first = (stage_row < stage_col) | ((stage_row == stage_col) & (across < down))
        rank = jnp.sum(first.astype(jnp.int32), axis=1, keepdims=True)
        tab_v[ry : ry + 1, :R] = jnp.sum(jnp.where(rank == across, code, 0), axis=0, keepdims=True)

    def stored(ry, i, which):
        parts = []
        for b in range(PER):
            code = tab[ry, i * PER + b]
            parts.append(kvc[(code & 255) >> 1, which, code & 1])
        return jnp.concatenate(parts, axis=0)

    causal = lax.broadcasted_iota(jnp.int32, (SEG, SEG), 0) >= lax.broadcasted_iota(jnp.int32, (SEG, SEG), 1)

    def forward_near(ry):
        q = q4[ry]
        s_own = jnp.where(causal, dot_nt(q, near(ry, 0)), NEG)
        s_near[ry, 0] = s_own
        dead = (1 - jnp.minimum(seg_id(ry), 1)).astype(F32)
        s_cache = dot_nt(q, near(cache_slot(ry), 0)) + dead * NEG
        s_near[ry, 1] = s_cache
        top = fold(fold(s_own[:, :DH], s_own[:, DH:], jnp.maximum), s_cache, jnp.maximum)
        top = jnp.broadcast_to(jnp.max(top, axis=1, keepdims=True), (SEG, DH))
        total = jnp.zeros((SEG, DH), F32)
        mixed = jnp.zeros((SEG, DH), F32)
        wide_top = jnp.concatenate([top] * (SEG // DH), axis=1)
        for s, at in ((s_own, ry), (s_cache, cache_slot(ry))):
            p = jnp.exp2((s - wide_top) * scale2)
            total = fold(total, p, jnp.add)
            mixed += dot_nn(p.astype(BF16), near(at, 1))
        top4[ry], sum4[ry], mix4[ry] = top, total, mixed

    def forward_mem(i):
        def pair(n, _):
            rys = [n * 2, n * 2 + 1]
            scores = [dot_nt(q4[ry], stored(ry, i, 0)) for ry in rys]
            for ry, s in zip(rys, scores):
                if i * PER < R - SURE:
                    parts = []
                    for b in range(PER):
                        dead = (tab[ry, i * PER + b] >> 8).astype(F32)
                        parts.append(s[:, b * BLOCK : (b + 1) * BLOCK] + dead * NEG)
                    s = jnp.concatenate(parts, axis=1)
                old = top4[ry]
                top = jnp.max(fold(s[:, :DH], s[:, DH:], jnp.maximum), axis=1, keepdims=True)
                top = jnp.maximum(old, jnp.broadcast_to(top, (SEG, DH)))
                less = jnp.exp2((old - top) * scale2)
                p = jnp.exp2((s - jnp.concatenate([top] * (WIDE // DH), axis=1)) * scale2)
                sum4[ry] = fold(sum4[ry] * less, p, jnp.add)
                p = p.astype(BF16)
                p_mem[ry, i] = p
                mix4[ry] = mix4[ry] * less + dot_nn(p, stored(ry, i, 1))
                top4[ry] = top
                m_mem[ry, i] = top
            return _

        lax.fori_loop(0, NY // 2, pair, 0)

    def finish(ry):
        inv = 1.0 / jnp.sum(sum4[ry], axis=1, keepdims=True)
        attn = (mix4[ry] * inv).astype(BF16)
        attn4[ry] = attn
        delta = jnp.sum(do4[ry].astype(F32) * attn.astype(F32), axis=1, keepdims=True)
        stat[ry, 0] = top4[ry]
        stat[ry, 1] = jnp.broadcast_to(inv, (SEG, DH))
        stat[ry, 2] = jnp.broadcast_to(delta, (SEG, DH))

    lower, upper = pl.ds(0, SEG // 2), pl.ds(SEG // 2, SEG // 2)
    width = g4.shape[3]

    def x_first(ry):
        arrived(g4.at[ry, x], gs.at[ry - 1], gr.at[ry - 1])
        send(g4.at[ry, x], g4.at[ry, x], xs.at[ry, 0], xr.at[ry, 0], x_peer[1])
        send(g4.at[ry, x], g4.at[ry, x], xs.at[ry, 1], xr.at[ry, 1], x_peer[NX - 1])

    def x_second(ry):
        left, right = x_of[NX - 1], x_of[1]
        arrived(g4.at[ry, left], xs.at[ry, 0], xr.at[ry, 0])
        send(g4.at[ry, left, lower], g4.at[ry, left, lower], xs.at[ry, 2], xr.at[ry, 2], x_peer[1])
        arrived(g4.at[ry, right], xs.at[ry, 1], xr.at[ry, 1])
        send(g4.at[ry, right, upper], g4.at[ry, right, upper], xs.at[ry, 3], xr.at[ry, 3], x_peer[NX - 1])

    def d_attn(ry):
        arrived(g4.at[ry, x_of[2], lower], xs.at[ry, 2], xr.at[ry, 2])
        arrived(g4.at[ry, x_of[2], upper], xs.at[ry, 3], xr.at[ry, 3])
        da = jnp.zeros((SEG, DH), F32)
        for i in range(NX):
            da += dot_nt(g4[ry, i], w_v[cols(y), i * width : (i + 1) * width])
        do4[ry] = da.astype(BF16)

    def g_send(d):
        send(g_ref, g4.at[NY - d, x], gs.at[d - 1], gr.at[NY - d - 1], y_peer[d])

    z_part(0, 0)
    z_part(1, 0)
    z_part(0, 1)
    z_part(0, 3)
    for d in (3, 1, 2):
        g_send(d)
    x_second(0)
    z_part(0, 2)
    for d in (1, 3, 2):
        send(q_ref.at[:, cols(y_of[d])], q4.at[NY - d], ys.at[d - 1, 2], yr.at[NY - d - 1, 2], y_peer[d])
    z_part(2, 0)
    for ry in range(NY):
        make_table(ry)
    to_smem = pltpu.make_async_copy(tab_v, tab, loc.at[0])
    to_smem.start()
    z_part(1, 1)
    weights_in.wait()
    z_part(1, 3)
    d_attn(0)
    z_part(1, 2)
    x_first(1)
    x_first(3)
    to_smem.wait()
    for ry in range(1, NY):
        arrived(q4.at[ry], ys.at[ry - 1, 2], yr.at[ry - 1, 2])
    for ry in order:
        take(0, ry)
    for ry in order:
        take(NZ - 1, ry)

    def near_step(ry, _):
        forward_near(ry)
        return _

    lax.fori_loop(0, NY, near_step, 0)
    z_part(3, 0)
    z_part(2, 1)
    x_first(2)
    z_part(2, 3)
    x_second(1)
    for ry in order:
        take(1, ry)
    z_part(2, 2)
    for rz in (NZ - 2, 2):
        for ry in order:
            take(rz, ry)
    forward_mem(0)
    x_second(3)
    z_far(0)
    forward_mem(1)
    take(NZ - 3, 0)
    take(3, 0)
    z_part(3, 1)
    forward_mem(2)
    take(NZ - 3, 1)
    take(3, 1)
    z_part(3, 3)
    forward_mem(3)
    take(NZ - 3, 3)
    take(3, 3)
    x_second(2)
    d_attn(1)
    z_part(3, 2)
    forward_mem(4)
    take(NZ - 3, 2)
    take(3, 2)
    z_far(1)
    forward_mem(5)
    take(NZ // 2, 0)
    take(NZ // 2, 1)
    z_far(3)
    d_attn(3)
    z_far(2)
    forward_mem(6)
    d_attn(2)
    take(NZ // 2, 3)
    take(NZ // 2, 2)
    forward_mem(7)

    def backward_near(ry):
        q, do = q4[ry], do4[ry]
        top, inv, delta = stat[ry, 0, :, :1], stat[ry, 1, :, :1], stat[ry, 2, :, :1]
        dq = jnp.zeros((SEG, DH), F32)
        for part, at in ((0, ry), (1, cache_slot(ry))):
            weights = jnp.exp2((s_near[ry, part] - top) * scale2) * inv
            slopes = (weights * (dot_nt(do, near(at, 1)) - delta)).astype(BF16)
            dq += dot_nn(slopes, near(at, 0))
            gk_part = dot_tn(slopes, q) * scale
            gv_part = dot_tn(weights.astype(BF16), do)
            if part == 0:
                near_acc[ry, 0] = gk_part
                near_acc[ry, 1] = gv_part
            else:
                carry_out[ry, 0] = gk_part.astype(BF16)
                carry_out[ry, 1] = gv_part.astype(BF16)
        dq_acc[ry] = dq

    def backward_mem(ry):
        do = do4[ry]
        top, inv, delta = stat[ry, 0], stat[ry, 1], stat[ry, 2]
        wide_delta = jnp.concatenate([delta] * (WIDE // DH), axis=1)

        def step(n, dq):
            for i in [4 * n + k for k in range(4)]:
                slopes = (p_mem[ry, i].astype(F32) * (dot_nt(do, stored(ry, i, 1)) - wide_delta)).astype(BF16)
                dq += dot_nn(slopes, stored(ry, i, 0)) * jnp.exp2((m_mem[ry, i] - top) * scale2)
            return dq

        dq = lax.fori_loop(0, CHUNKS // 4, step, jnp.zeros((SEG, DH), F32))
        gq[ry] = ((dq_acc[ry] + dq * inv) * scale).astype(BF16)

    for n, ry in enumerate((2, 1, 3, 0)):
        finish(ry)
        if ry:
            send(attn4.at[ry], attn_in.at[y], as_.at[ry - 1], ar.at[ry - 1], y_peer[ry])
        turned = attn4[ry].T
        for i in range(NX):
            part = dot_nn(turned, g4[ry, i])
            pt[i] = part if n == 0 else pt[i] + part
    attn_in[y] = attn4[0]

    rows = pg_ref.shape[0]
    for i in range(NY):
        pp[i] = pt[i].T.astype(BF16).reshape(NZ, NC, rows, DH)
        send(pp.at[i, :, 1 - c], rs0.at[i], bs.at[i], br.at[i], sibling)
    for ry in range(NY):
        backward_near(ry)
        to = lax.rem(ry + NY - wrap, NY)
        send(carry_out.at[ry], carry_in.at[to], cs.at[ry], cr.at[to], back)
    for i in range(NY):
        arrived(rs0.at[i], bs.at[i], br.at[i])
        r1[:, i] = (pp[i, :, c].astype(F32) + rs0[i].astype(F32)).astype(BF16)
    for d in (4, 3, 5, 2, 6, 1, 7):
        send(r1.at[z_of[d]], rs2.at[d - 1], rzs.at[d - 1], rzr.at[d - 1], z_peer[d])

    for d in (1, 3, 2):
        arrived(attn_in.at[y_of[NY - d]], as_.at[d - 1], ar.at[d - 1])
    attn = jnp.concatenate([attn_in[i] for i in range(NY)], axis=1)
    for i in range(NX):
        lo_out[i] = dot_nn(attn, w_v[:, i * width : (i + 1) * width]).astype(BF16)
    for d in (2, 1, 3):
        send(lo_out.at[x_of[d]], lo_in.at[d - 1], ls.at[d - 1], lr.at[d - 1], x_peer[d])
    backward_mem(2)
    send(gq.at[2], dq_ref.at[:, cols(y)], os_.at[0, 1], or_.at[0, 1], y_peer[2])
    for ry in (2, 1, 3, 0):
        arrived(carry_in.at[ry], cs.at[ry], cr.at[ry])
        gk[ry] = (near_acc[ry, 0] + carry_in[ry, 0].astype(F32)).astype(BF16)
        gv[ry] = (near_acc[ry, 1] + carry_in[ry, 1].astype(F32)).astype(BF16)
        if ry:
            send(gk.at[ry], dk_ref.at[:, cols(y)], os_.at[1, ry - 1], or_.at[1, ry - 1], y_peer[ry])
            send(gv.at[ry], dv_ref.at[:, cols(y)], os_.at[2, ry - 1], or_.at[2, ry - 1], y_peer[ry])
    backward_mem(1)
    send(gq.at[1], dq_ref.at[:, cols(y)], os_.at[0, 0], or_.at[0, 0], y_peer[1])
    total = r1[z].astype(F32)
    for d in range(1, NZ):
        arrived(rs2.at[d - 1], rzs.at[d - 1], rzr.at[d - 1])
        total += rs2[d - 1].astype(F32)
    r2[...] = total
    for d in (2, 1, 3):
        send(r2.at[y_of[d]], pg_ref.at[:, cols(y)], ps.at[d - 1], pr.at[d - 1], y_peer[d])
    backward_mem(3)
    send(gq.at[3], dq_ref.at[:, cols(y)], os_.at[0, 2], or_.at[0, 2], y_peer[3])
    backward_mem(0)

    home = [
        pltpu.make_async_copy(gq.at[0], dq_ref.at[:, cols(y)], loc.at[0]),
        pltpu.make_async_copy(gk.at[0], dk_ref.at[:, cols(y)], loc.at[1]),
        pltpu.make_async_copy(gv.at[0], dv_ref.at[:, cols(y)], loc.at[2]),
        pltpu.make_async_copy(r2.at[y], pg_ref.at[:, cols(y)], loc.at[5]),
    ]
    for copy in home:
        copy.start()
    out = lo_out[x].astype(F32)
    for d in range(1, NX):
        arrived(lo_in.at[d - 1], ls.at[d - 1], lr.at[d - 1])
        out += lo_in[d - 1].astype(F32)
    lo_v[...] = out.astype(BF16)
    home.append(pltpu.make_async_copy(lo_v, lo_ref, loc.at[3]))
    home[-1].start()
    for d in range(1, NY):
        arrived(pg_ref.at[:, cols(y_of[NY - d])], ps.at[d - 1], pr.at[d - 1])
    for n, ref in enumerate((dq_ref, dk_ref, dv_ref)):
        for d in range(1, NY):
            arrived(ref.at[:, cols(y_of[NY - d])], os_.at[n, d - 1], or_.at[n, d - 1])
    for copy in home:
        copy.wait()
    for copy in sends:
        copy.wait_send()


def hand_over(*refs):
    for i in range(5):
        refs[5 + i][...] = refs[i][...]


def per_device(queries, keys, values, out_grad, out_weight, retr_owner, retr_block):
    tok, wide = queries.shape
    full = out_weight.shape[1]
    rows = full // (NY * NZ * NC)
    vmem = pl.BlockSpec(memory_space=pltpu.VMEM)
    anywhere = pl.BlockSpec(memory_space=pl.ANY)
    dma = pltpu.SemaphoreType.DMA
    tile = (tok, DH)
    halves = tok // BLOCK
    scratch = [
        pltpu.VMEM((wide, full), BF16),
        pltpu.VMEM((tok, wide), BF16),
        pltpu.VMEM((NC * NZ * NY, 2, halves, BLOCK, DH), BF16),
        pltpu.VMEM((NC * NZ * NY, 2, halves, BLOCK, DH), BF16),
        pltpu.VMEM((NY,) + tile, BF16),
        pltpu.VMEM((NY,) + tile, BF16),
        pltpu.VMEM((NY, NX, tok, wide), BF16),
        pltpu.VMEM((NY, 2, tok, tok), F32),
        pltpu.VMEM((NY, CHUNKS, tok, WIDE), BF16),
        pltpu.VMEM((NY, CHUNKS) + tile, F32),
        pltpu.VMEM((NY,) + tile, F32),
        pltpu.VMEM((NY,) + tile, F32),
        pltpu.VMEM((NY,) + tile, F32),
        pltpu.VMEM((NY, 3) + tile, F32),
        pltpu.VMEM((NY,) + tile, BF16),
        pltpu.VMEM((NY,) + tile, BF16),
        pltpu.VMEM((NX, tok, wide), BF16),
        pltpu.VMEM((NX - 1, tok, wide), BF16),
        pltpu.VMEM((NX, DH, wide), F32),
        pltpu.VMEM((NY, NZ, NC, rows, DH), BF16),
        pltpu.VMEM((NY, NZ, rows, DH), BF16),
        pltpu.VMEM((NZ, NY, rows, DH), BF16),
        pltpu.VMEM((NZ - 1, NY, rows, DH), BF16),
        pltpu.VMEM((NY, rows, DH), F32),
        pltpu.VMEM((NY,) + tile, F32),
        pltpu.VMEM((NY, 2) + tile, F32),
        pltpu.VMEM((NY, 2) + tile, BF16),
        pltpu.VMEM((NY, 2) + tile, BF16),
        pltpu.VMEM((NY,) + tile, BF16),
        pltpu.VMEM((NY,) + tile, BF16),
        pltpu.VMEM((NY,) + tile, BF16),
        pltpu.VMEM((8, DH), jnp.int32),
        pltpu.SMEM((8, DH), jnp.int32),
        dma((6,)),
        dma((NY - 1, 3)), dma((NY - 1, 3)),
        dma((NY - 1,)), dma((NY - 1,)),
        dma((NY, 4)), dma((NY, 4)),
        dma((2, NZ // 2, NY)), dma((2, NZ // 2, NY)),
        dma((NZ, NY)), dma((NZ, NY)),
        dma((NY - 1,)), dma((NY - 1,)),
        dma((NY,)), dma((NY,)),
        dma((NY,)), dma((NY,)),
        dma((NZ - 1,)), dma((NZ - 1,)),
        dma((NX - 1,)), dma((NX - 1,)),
        dma((NY - 1,)), dma((NY - 1,)),
        dma((3, NY - 1)), dma((3, NY - 1)),
    ]
    grad = jax.ShapeDtypeStruct((tok, wide), BF16)
    shapes = (grad, grad, grad, grad, jax.ShapeDtypeStruct((rows, wide), F32))
    results = pl.pallas_call(
        kernel,
        out_shape=shapes,
        in_specs=[vmem] * 2 + [anywhere] * 5,
        out_specs=(anywhere,) * 5,
        scratch_shapes=scratch,
        compiler_params=pltpu.CompilerParams(
            collective_id=0, has_side_effects=True, vmem_limit_bytes=60 * 1024 * 1024
        ),
    )(
        retr_owner.T,
        retr_block.T,
        queries,
        keys.reshape(halves, BLOCK, wide),
        values.reshape(halves, BLOCK, wide),
        out_grad,
        out_weight,
    )
    return pl.pallas_call(hand_over, out_shape=shapes, in_specs=[vmem] * 5, out_specs=(vmem,) * 5)(*results)


def solution(mesh):
    rows = P("seg", "head")
    return jax.shard_map(
        per_device,
        mesh=mesh,
        in_specs=(rows, rows, rows, rows, P("head", None), P(), P()),
        out_specs=(rows,) * 5,
        check_vma=False,
    )
```

```python
import math

import jax
import jax.numpy as jnp
from jax import lax
from jax.experimental import pallas as pl
from jax.experimental.pallas import tpu as pltpu
from jax.sharding import PartitionSpec as P

DH = 128
BLOCK = 128
SEG = 256
R = 32
NY, NZ, NC, NX = 4, 8, 2, 4
MESH = pl.DeviceIdType.MESH
F32, BF16 = jnp.float32, jnp.bfloat16
NEG = -1e30
SURE = 24
PER = 4
WIDE = PER * BLOCK
CHUNKS = R // PER


def dot_nt(a, b):
    return lax.dot_general(a, b, (((1,), (1,)), ((), ())), preferred_element_type=F32)


def dot_nn(a, b):
    return lax.dot_general(a, b, (((1,), (0,)), ((), ())), preferred_element_type=F32)


def dot_tn(a, b):
    return lax.dot_general(a, b, (((0,), (0,)), ((), ())), preferred_element_type=F32)


def kernel(
    owner_ref, block_ref, q_ref, k_ref, v_ref, g_ref, w_ref,
    lo_ref, dq_ref, dk_ref, dv_ref, pg_ref,
    w_v, lo_v, kv, kvc, q4, do4, g4, s_near, p_mem, m_mem, top4, sum4, mix4, stat, attn4, attn_in, lo_out, lo_in,
    pp, rs0, r1, rs2, r2, dq_acc, near_acc, carry_out, carry_in, gq, gk, gv, tab_v, tab,
    loc, ys, yr, gs, gr, xs, xr, zs, zr, ms, mr, as_, ar, bs, br, cs, cr, rzs, rzr, ls, lr, ps, pr, os_, or_,
):
    s_me = lax.axis_index("seg")
    x = lax.axis_index("head")
    c = lax.rem(s_me, NC)
    z = lax.rem(lax.div(s_me, NC), NZ)
    y = lax.div(s_me, NC * NZ)
    scale = 1.0 / math.sqrt(DH)
    scale2 = scale * math.log2(math.e)

    def seg_of(yy, zz, cc):
        return (yy * NZ + zz) * NC + cc

    y_of = [lax.rem(y + d, NY) for d in range(NY)]
    x_of = [lax.rem(x + d, NX) for d in range(NX)]
    z_of = [lax.rem(z + d, NZ) for d in range(NZ)]
    y_peer = [(seg_of(y_of[d], z, c), x) for d in range(NY)]
    z_peer = [(seg_of(y, z_of[d], c), x) for d in range(NZ)]
    x_peer = [(s_me, x_of[d]) for d in range(NX)]
    sibling = (seg_of(y, z, 1 - c), x)
    cross = (seg_of(y, lax.rem(z + NZ - 1 + 2 * c, NZ), 1 - c), x)
    back = (seg_of(y, lax.rem(z + NZ - 1 + c, NZ), 1 - c), x)
    wrap = 1 - jnp.minimum(z + c, 1)

    sends = []

    def send(src, dst, ssem, rsem, dev):
        copy = pltpu.make_async_remote_copy(
            src_ref=src, dst_ref=dst, send_sem=ssem, recv_sem=rsem, device_id=dev, device_id_type=MESH
        )
        copy.start()
        sends.append(copy)

    def arrived(dst, ssem, rsem):
        pltpu.make_async_remote_copy(
            src_ref=dst, dst_ref=dst, send_sem=ssem, recv_sem=rsem, device_id=sibling, device_id_type=MESH
        ).wait_recv()

    def cols(i):
        return pl.ds(pl.multiple_of(i * DH, DH), DH)

    def slot(plane, rz, ry):
        return (plane * NZ + rz) * NY + ry

    own = [
        pltpu.make_async_copy(k_ref.at[:, :, cols(y)], kv.at[0, 0], loc.at[0]),
        pltpu.make_async_copy(v_ref.at[:, :, cols(y)], kv.at[0, 1], loc.at[1]),
        pltpu.make_async_copy(q_ref.at[:, cols(y)], q4.at[0], loc.at[2]),
        pltpu.make_async_copy(g_ref, g4.at[0, x], loc.at[3]),
    ]
    weights_in = pltpu.make_async_copy(w_ref, w_v, loc.at[4])
    for copy in own + [weights_in]:
        copy.start()

    barrier = pltpu.get_barrier_semaphore()
    peers = y_peer[1:] + z_peer[1:] + x_peer[1:] + [sibling, cross]
    for dev in peers:
        pl.semaphore_signal(barrier, inc=1, device_id=dev, device_id_type=MESH)
    pl.semaphore_wait(barrier, len(peers))

    for d in (1, 3, 2):
        send(k_ref.at[:, :, cols(y_of[d])], kv.at[NY - d, 0], ys.at[d - 1, 0], yr.at[NY - d - 1, 0], y_peer[d])
        send(v_ref.at[:, :, cols(y_of[d])], kv.at[NY - d, 1], ys.at[d - 1, 1], yr.at[NY - d - 1, 1], y_peer[d])
    send(g_ref, g4.at[0, x], xs.at[0, 0], xr.at[0, 0], x_peer[1])
    send(g_ref, g4.at[0, x], xs.at[0, 1], xr.at[0, 1], x_peer[NX - 1])
    for copy in own:
        copy.wait()
    order = (0, 1, 3, 2)

    def z_part(t, ry):
        up, down = (NZ - t) % NZ, t
        if t == 0:
            if ry:
                arrived(kv.at[ry, 0], ys.at[ry - 1, 0], yr.at[ry - 1, 0])
                arrived(kv.at[ry, 1], ys.at[ry - 1, 1], yr.at[ry - 1, 1])
        else:
            arrived(kv.at[slot(0, up, ry)], zs.at[0, t - 1, ry], zr.at[0, t - 1, ry])
            arrived(kv.at[slot(0, down, ry)], zs.at[1, t - 1, ry], zr.at[1, t - 1, ry])
        if t < NZ // 2 - 1:
            send(kv.at[slot(0, up, ry)], kv.at[slot(0, NZ - 1 - t, ry)], zs.at[0, t, ry], zr.at[0, t, ry], z_peer[1])
            send(kv.at[slot(0, down, ry)], kv.at[slot(0, t + 1, ry)], zs.at[1, t, ry], zr.at[1, t, ry], z_peer[NZ - 1])
        else:
            far = slot(0, NZ // 2, ry)
            send(kv.at[slot(0, up, ry), 0], kv.at[far, 0], zs.at[0, t, ry], zr.at[0, t, ry], z_peer[1])
            send(kv.at[slot(0, down, ry), 1], kv.at[far, 1], zs.at[1, t, ry], zr.at[1, t, ry], z_peer[NZ - 1])
        for rz in ((0,) if t == 0 else (up, down)):
            send(kv.at[slot(0, rz, ry)], kv.at[slot(1, rz, ry)], ms.at[rz, ry], mr.at[rz, ry], sibling)

    def z_far(ry):
        far, t = slot(0, NZ // 2, ry), NZ // 2 - 1
        arrived(kv.at[far, 0], zs.at[0, t, ry], zr.at[0, t, ry])
        arrived(kv.at[far, 1], zs.at[1, t, ry], zr.at[1, t, ry])
        send(kv.at[far], kv.at[slot(1, NZ // 2, ry)], ms.at[NZ // 2, ry], mr.at[NZ // 2, ry], sibling)

    def take(rz, ry):
        arrived(kv.at[slot(1, rz, ry)], ms.at[rz, ry], mr.at[rz, ry])
        for plane in range(NC):
            kvc[slot(plane, rz, ry)] = kv[slot(plane, rz, ry)]

    def seg_id(ry):
        return seg_of(lax.rem(y + ry, NY), z, c)

    def cache_slot(ry):
        return slot(1, (NZ - 1) * (1 - c), lax.rem(ry + NY - wrap, NY))

    def near(at, which):
        return kvc[at, which].reshape(SEG, DH)

    def fold(m, entry, op):
        for i in range(entry.shape[1] // DH):
            m = op(m, entry[:, i * DH : (i + 1) * DH])
        return m

    def make_table(ry):
        lane = lax.broadcasted_iota(jnp.int32, owner_ref.shape, 1) == seg_id(ry)
        o = jnp.sum(jnp.where(lane, owner_ref[...], 0), axis=1, keepdims=True)
        b = jnp.sum(jnp.where(lane, block_ref[...], 0), axis=1, keepdims=True)
        rz = ((o >> 1) & (NZ - 1)) + NZ - z & (NZ - 1)
        rr = (o >> 4) + NY - y & (NY - 1)
        plane = (o + c) & (NC - 1)
        away = jnp.minimum(rz, NZ - rz)
        dead = b < 0
        turn = rr ^ (rr >> 1)
        stage = jnp.where(away < 3, 0, jnp.where(away == 3, 1 + turn, 1 + NY + turn))
        stage = jnp.where(dead, -1, stage)
        code = jnp.where(dead, 256, ((plane * NZ + rz) * NY + rr) * 2 + jnp.maximum(b, 0))
        down = lax.broadcasted_iota(jnp.int32, (R, R), 0)
        across = lax.broadcasted_iota(jnp.int32, (R, R), 1)
        stage_col = jnp.broadcast_to(stage, (R, R))
        stage_row = jnp.sum(jnp.where(down == across, stage_col, 0), axis=0, keepdims=True)
        first = (stage_row < stage_col) | ((stage_row == stage_col) & (across < down))
        rank = jnp.sum(first.astype(jnp.int32), axis=1, keepdims=True)
        tab_v[ry : ry + 1, :R] = jnp.sum(jnp.where(rank == across, code, 0), axis=0, keepdims=True)

    def stored(ry, i, which):
        parts = []
        for b in range(PER):
            code = tab[ry, i * PER + b]
            parts.append(kvc[(code & 255) >> 1, which, code & 1])
        return jnp.concatenate(parts, axis=0)

    causal = lax.broadcasted_iota(jnp.int32, (SEG, SEG), 0) >= lax.broadcasted_iota(jnp.int32, (SEG, SEG), 1)

    def forward_near(ry):
        q = q4[ry]
        s_own = jnp.where(causal, dot_nt(q, near(ry, 0)), NEG)
        s_near[ry, 0] = s_own
        dead = (1 - jnp.minimum(seg_id(ry), 1)).astype(F32)
        s_cache = dot_nt(q, near(cache_slot(ry), 0)) + dead * NEG
        s_near[ry, 1] = s_cache
        top = fold(fold(s_own[:, :DH], s_own[:, DH:], jnp.maximum), s_cache, jnp.maximum)
        top = jnp.broadcast_to(jnp.max(top, axis=1, keepdims=True), (SEG, DH))
        total = jnp.zeros((SEG, DH), F32)
        mixed = jnp.zeros((SEG, DH), F32)
        wide_top = jnp.concatenate([top] * (SEG // DH), axis=1)
        for s, at in ((s_own, ry), (s_cache, cache_slot(ry))):
            p = jnp.exp2((s - wide_top) * scale2)
            total = fold(total, p, jnp.add)
            mixed += dot_nn(p.astype(BF16), near(at, 1))
        top4[ry], sum4[ry], mix4[ry] = top, total, mixed

    def forward_mem(i):
        def pair(n, _):
            rys = [n * 2, n * 2 + 1]
            scores = [dot_nt(q4[ry], stored(ry, i, 0)) for ry in rys]
            for ry, s in zip(rys, scores):
                if i * PER < R - SURE:
                    parts = []
                    for b in range(PER):
                        dead = (tab[ry, i * PER + b] >> 8).astype(F32)
                        parts.append(s[:, b * BLOCK : (b + 1) * BLOCK] + dead * NEG)
                    s = jnp.concatenate(parts, axis=1)
                old = top4[ry]
                top = jnp.max(fold(s[:, :DH], s[:, DH:], jnp.maximum), axis=1, keepdims=True)
                top = jnp.maximum(old, jnp.broadcast_to(top, (SEG, DH)))
                less = jnp.exp2((old - top) * scale2)
                p = jnp.exp2((s - jnp.concatenate([top] * (WIDE // DH), axis=1)) * scale2)
                sum4[ry] = fold(sum4[ry] * less, p, jnp.add)
                p = p.astype(BF16)
                p_mem[ry, i] = p
                mix4[ry] = mix4[ry] * less + dot_nn(p, stored(ry, i, 1))
                top4[ry] = top
                m_mem[ry, i] = top
            return _

        lax.fori_loop(0, NY // 2, pair, 0)

    def finish(ry):
        inv = 1.0 / jnp.sum(sum4[ry], axis=1, keepdims=True)
        attn = (mix4[ry] * inv).astype(BF16)
        attn4[ry] = attn
        delta = jnp.sum(do4[ry].astype(F32) * attn.astype(F32), axis=1, keepdims=True)
        stat[ry, 0] = top4[ry]
        stat[ry, 1] = jnp.broadcast_to(inv, (SEG, DH))
        stat[ry, 2] = jnp.broadcast_to(delta, (SEG, DH))

    lower, upper = pl.ds(0, SEG // 2), pl.ds(SEG // 2, SEG // 2)
    width = g4.shape[3]

    def x_first(ry):
        arrived(g4.at[ry, x], gs.at[ry - 1], gr.at[ry - 1])
        send(g4.at[ry, x], g4.at[ry, x], xs.at[ry, 0], xr.at[ry, 0], x_peer[1])
        send(g4.at[ry, x], g4.at[ry, x], xs.at[ry, 1], xr.at[ry, 1], x_peer[NX - 1])

    def x_second(ry):
        left, right = x_of[NX - 1], x_of[1]
        arrived(g4.at[ry, left], xs.at[ry, 0], xr.at[ry, 0])
        send(g4.at[ry, left, lower], g4.at[ry, left, lower], xs.at[ry, 2], xr.at[ry, 2], x_peer[1])
        arrived(g4.at[ry, right], xs.at[ry, 1], xr.at[ry, 1])
        send(g4.at[ry, right, upper], g4.at[ry, right, upper], xs.at[ry, 3], xr.at[ry, 3], x_peer[NX - 1])

    def d_attn(ry):
        arrived(g4.at[ry, x_of[2], lower], xs.at[ry, 2], xr.at[ry, 2])
        arrived(g4.at[ry, x_of[2], upper], xs.at[ry, 3], xr.at[ry, 3])
        da = jnp.zeros((SEG, DH), F32)
        for i in range(NX):
            da += dot_nt(g4[ry, i], w_v[cols(y), i * width : (i + 1) * width])
        do4[ry] = da.astype(BF16)

    def g_send(d):
        send(g_ref, g4.at[NY - d, x], gs.at[d - 1], gr.at[NY - d - 1], y_peer[d])

    z_part(0, 0)
    z_part(1, 0)
    z_part(0, 1)
    z_part(0, 3)
    for d in (3, 1, 2):
        g_send(d)
    x_second(0)
    z_part(0, 2)
    for d in (1, 3, 2):
        send(q_ref.at[:, cols(y_of[d])], q4.at[NY - d], ys.at[d - 1, 2], yr.at[NY - d - 1, 2], y_peer[d])
    z_part(2, 0)
    for ry in range(NY):
        make_table(ry)
    to_smem = pltpu.make_async_copy(tab_v, tab, loc.at[0])
    to_smem.start()
    z_part(1, 1)
    weights_in.wait()
    z_part(1, 3)
    d_attn(0)
    z_part(1, 2)
    x_first(1)
    x_first(3)
    to_smem.wait()
    for ry in range(1, NY):
        arrived(q4.at[ry], ys.at[ry - 1, 2], yr.at[ry - 1, 2])
    for ry in order:
        take(0, ry)
    for ry in order:
        take(NZ - 1, ry)

    def near_step(ry, _):
        forward_near(ry)
        return _

    lax.fori_loop(0, NY, near_step, 0)
    z_part(3, 0)
    z_part(2, 1)
    x_first(2)
    z_part(2, 3)
    x_second(1)
    for ry in order:
        take(1, ry)
    z_part(2, 2)
    for rz in (NZ - 2, 2):
        for ry in order:
            take(rz, ry)
    forward_mem(0)
    x_second(3)
    z_far(0)
    forward_mem(1)
    take(NZ - 3, 0)
    take(3, 0)
    z_part(3, 1)
    forward_mem(2)
    take(NZ - 3, 1)
    take(3, 1)
    z_part(3, 3)
    forward_mem(3)
    take(NZ - 3, 3)
    take(3, 3)
    x_second(2)
    d_attn(1)
    z_part(3, 2)
    forward_mem(4)
    take(NZ - 3, 2)
    take(3, 2)
    z_far(1)
    forward_mem(5)
    take(NZ // 2, 0)
    take(NZ // 2, 1)
    z_far(3)
    d_attn(3)
    z_far(2)
    forward_mem(6)
    d_attn(2)
    take(NZ // 2, 3)
    take(NZ // 2, 2)
    forward_mem(7)

    def backward_near(ry):
        q, do = q4[ry], do4[ry]
        top, inv, delta = stat[ry, 0, :, :1], stat[ry, 1, :, :1], stat[ry, 2, :, :1]
        dq = jnp.zeros((SEG, DH), F32)
        for part, at in ((0, ry), (1, cache_slot(ry))):
            weights = jnp.exp2((s_near[ry, part] - top) * scale2) * inv
            slopes = (weights * (dot_nt(do, near(at, 1)) - delta)).astype(BF16)
            dq += dot_nn(slopes, near(at, 0))
            gk_part = dot_tn(slopes, q) * scale
            gv_part = dot_tn(weights.astype(BF16), do)
            if part == 0:
                near_acc[ry, 0] = gk_part
                near_acc[ry, 1] = gv_part
            else:
                carry_out[ry, 0] = gk_part.astype(BF16)
                carry_out[ry, 1] = gv_part.astype(BF16)
        dq_acc[ry] = dq

    def backward_mem(ry):
        do = do4[ry]
        top, inv, delta = stat[ry, 0], stat[ry, 1], stat[ry, 2]
        wide_delta = jnp.concatenate([delta] * (WIDE // DH), axis=1)

        def step(n, dq):
            for i in [4 * n + k for k in range(4)]:
                slopes = p_mem[ry, i] * (dot_nt(do, stored(ry, i, 1)) - wide_delta).astype(BF16)
                dq += dot_nn(slopes, stored(ry, i, 0)) * jnp.exp2((m_mem[ry, i] - top) * scale2)
            return dq

        dq = lax.fori_loop(0, CHUNKS // 4, step, jnp.zeros((SEG, DH), F32))
        gq[ry] = ((dq_acc[ry] + dq * inv) * scale).astype(BF16)

    for ry in (2, 1, 3, 0):
        finish(ry)
        if ry:
            send(attn4.at[ry], attn_in.at[y], as_.at[ry - 1], ar.at[ry - 1], y_peer[ry])
    attn_in[y] = attn4[0]

    rows = pg_ref.shape[0]
    turned = jnp.concatenate([attn4[ry].T for ry in range(NY)], axis=1)
    for i in range(NY):
        part = dot_nn(turned, g4[:, i].reshape(NY * SEG, width))
        pp[i] = part.T.astype(BF16).reshape(NZ, NC, rows, DH)
        send(pp.at[i, :, 1 - c], rs0.at[i], bs.at[i], br.at[i], sibling)
    for ry in range(NY):
        backward_near(ry)
        to = lax.rem(ry + NY - wrap, NY)
        send(carry_out.at[ry], carry_in.at[to], cs.at[ry], cr.at[to], back)
    for i in range(NY):
        arrived(rs0.at[i], bs.at[i], br.at[i])
        r1[:, i] = (pp[i, :, c].astype(F32) + rs0[i].astype(F32)).astype(BF16)
    for d in (4, 3, 5, 2, 6, 1, 7):
        send(r1.at[z_of[d]], rs2.at[d - 1], rzs.at[d - 1], rzr.at[d - 1], z_peer[d])

    for d in (1, 3, 2):
        arrived(attn_in.at[y_of[NY - d]], as_.at[d - 1], ar.at[d - 1])
    attn = jnp.concatenate([attn_in[i] for i in range(NY)], axis=1)
    for i in range(NX):
        lo_out[i] = dot_nn(attn, w_v[:, i * width : (i + 1) * width]).astype(BF16)
    for d in (2, 1, 3):
        send(lo_out.at[x_of[d]], lo_in.at[d - 1], ls.at[d - 1], lr.at[d - 1], x_peer[d])
    backward_mem(2)
    send(gq.at[2], dq_ref.at[:, cols(y)], os_.at[0, 1], or_.at[0, 1], y_peer[2])
    for ry in (2, 1, 3, 0):
        arrived(carry_in.at[ry], cs.at[ry], cr.at[ry])
        gk[ry] = (near_acc[ry, 0] + carry_in[ry, 0].astype(F32)).astype(BF16)
        gv[ry] = (near_acc[ry, 1] + carry_in[ry, 1].astype(F32)).astype(BF16)
        if ry:
            send(gk.at[ry], dk_ref.at[:, cols(y)], os_.at[1, ry - 1], or_.at[1, ry - 1], y_peer[ry])
            send(gv.at[ry], dv_ref.at[:, cols(y)], os_.at[2, ry - 1], or_.at[2, ry - 1], y_peer[ry])
    backward_mem(1)
    send(gq.at[1], dq_ref.at[:, cols(y)], os_.at[0, 0], or_.at[0, 0], y_peer[1])
    total = r1[z].astype(F32)
    for d in range(1, NZ):
        arrived(rs2.at[d - 1], rzs.at[d - 1], rzr.at[d - 1])
        total += rs2[d - 1].astype(F32)
    r2[...] = total
    for d in (2, 1, 3):
        send(r2.at[y_of[d]], pg_ref.at[:, cols(y)], ps.at[d - 1], pr.at[d - 1], y_peer[d])
    backward_mem(3)
    send(gq.at[3], dq_ref.at[:, cols(y)], os_.at[0, 2], or_.at[0, 2], y_peer[3])
    backward_mem(0)

    home = [
        pltpu.make_async_copy(gq.at[0], dq_ref.at[:, cols(y)], loc.at[0]),
        pltpu.make_async_copy(gk.at[0], dk_ref.at[:, cols(y)], loc.at[1]),
        pltpu.make_async_copy(gv.at[0], dv_ref.at[:, cols(y)], loc.at[2]),
        pltpu.make_async_copy(r2.at[y], pg_ref.at[:, cols(y)], loc.at[5]),
    ]
    for copy in home:
        copy.start()
    out = lo_out[x].astype(F32)
    for d in range(1, NX):
        arrived(lo_in.at[d - 1], ls.at[d - 1], lr.at[d - 1])
        out += lo_in[d - 1].astype(F32)
    lo_v[...] = out.astype(BF16)
    home.append(pltpu.make_async_copy(lo_v, lo_ref, loc.at[3]))
    home[-1].start()
    for d in range(1, NY):
        arrived(pg_ref.at[:, cols(y_of[NY - d])], ps.at[d - 1], pr.at[d - 1])
    for n, ref in enumerate((dq_ref, dk_ref, dv_ref)):
        for d in range(1, NY):
            arrived(ref.at[:, cols(y_of[NY - d])], os_.at[n, d - 1], or_.at[n, d - 1])
    for copy in home:
        copy.wait()
    for copy in sends:
        copy.wait_send()


def hand_over(*refs):
    for i in range(5):
        refs[5 + i][...] = refs[i][...]


def per_device(queries, keys, values, out_grad, out_weight, retr_owner, retr_block):
    tok, wide = queries.shape
    full = out_weight.shape[1]
    rows = full // (NY * NZ * NC)
    vmem = pl.BlockSpec(memory_space=pltpu.VMEM)
    anywhere = pl.BlockSpec(memory_space=pl.ANY)
    dma = pltpu.SemaphoreType.DMA
    tile = (tok, DH)
    halves = tok // BLOCK
    scratch = [
        pltpu.VMEM((wide, full), BF16),
        pltpu.VMEM((tok, wide), BF16),
        pltpu.VMEM((NC * NZ * NY, 2, halves, BLOCK, DH), BF16),
        pltpu.VMEM((NC * NZ * NY, 2, halves, BLOCK, DH), BF16),
        pltpu.VMEM((NY,) + tile, BF16),
        pltpu.VMEM((NY,) + tile, BF16),
        pltpu.VMEM((NY, NX, tok, wide), BF16),
        pltpu.VMEM((NY, 2, tok, tok), F32),
        pltpu.VMEM((NY, CHUNKS, tok, WIDE), BF16),
        pltpu.VMEM((NY, CHUNKS) + tile, F32),
        pltpu.VMEM((NY,) + tile, F32),
        pltpu.VMEM((NY,) + tile, F32),
        pltpu.VMEM((NY,) + tile, F32),
        pltpu.VMEM((NY, 3) + tile, F32),
        pltpu.VMEM((NY,) + tile, BF16),
        pltpu.VMEM((NY,) + tile, BF16),
        pltpu.VMEM((NX, tok, wide), BF16),
        pltpu.VMEM((NX - 1, tok, wide), BF16),
        pltpu.VMEM((NY, NZ, NC, rows, DH), BF16),
        pltpu.VMEM((NY, NZ, rows, DH), BF16),
        pltpu.VMEM((NZ, NY, rows, DH), BF16),
        pltpu.VMEM((NZ - 1, NY, rows, DH), BF16),
        pltpu.VMEM((NY, rows, DH), F32),
        pltpu.VMEM((NY,) + tile, F32),
        pltpu.VMEM((NY, 2) + tile, F32),
        pltpu.VMEM((NY, 2) + tile, BF16),
        pltpu.VMEM((NY, 2) + tile, BF16),
        pltpu.VMEM((NY,) + tile, BF16),
        pltpu.VMEM((NY,) + tile, BF16),
        pltpu.VMEM((NY,) + tile, BF16),
        pltpu.VMEM((8, DH), jnp.int32),
        pltpu.SMEM((8, DH), jnp.int32),
        dma((6,)),
        dma((NY - 1, 3)), dma((NY - 1, 3)),
        dma((NY - 1,)), dma((NY - 1,)),
        dma((NY, 4)), dma((NY, 4)),
        dma((2, NZ // 2, NY)), dma((2, NZ // 2, NY)),
        dma((NZ, NY)), dma((NZ, NY)),
        dma((NY - 1,)), dma((NY - 1,)),
        dma((NY,)), dma((NY,)),
        dma((NY,)), dma((NY,)),
        dma((NZ - 1,)), dma((NZ - 1,)),
        dma((NX - 1,)), dma((NX - 1,)),
        dma((NY - 1,)), dma((NY - 1,)),
        dma((3, NY - 1)), dma((3, NY - 1)),
    ]
    grad = jax.ShapeDtypeStruct((tok, wide), BF16)
    shapes = (grad, grad, grad, grad, jax.ShapeDtypeStruct((rows, wide), F32))
    results = pl.pallas_call(
        kernel,
        out_shape=shapes,
        in_specs=[vmem] * 2 + [anywhere] * 5,
        out_specs=(anywhere,) * 5,
        scratch_shapes=scratch,
        compiler_params=pltpu.CompilerParams(
            collective_id=0, has_side_effects=True, vmem_limit_bytes=60 * 1024 * 1024
        ),
    )(
        retr_owner.T,
        retr_block.T,
        queries,
        keys.reshape(halves, BLOCK, wide),
        values.reshape(halves, BLOCK, wide),
        out_grad,
        out_weight,
    )
    return pl.pallas_call(hand_over, out_shape=shapes, in_specs=[vmem] * 5, out_specs=(vmem,) * 5)(*results)


def solution(mesh):
    rows = P("seg", "head")
    return jax.shard_map(
        per_device,
        mesh=mesh,
        in_specs=(rows, rows, rows, rows, P("head", None), P(), P()),
        out_specs=(rows,) * 5,
        check_vma=False,
    )
```

```python
import math

import jax
import jax.numpy as jnp
from jax import lax
from jax.experimental import pallas as pl
from jax.experimental.pallas import tpu as pltpu
from jax.sharding import PartitionSpec as P

DH = 128
BLOCK = 128
SEG = 256
R = 32
NY, NZ, NC, NX = 4, 8, 2, 4
MESH = pl.DeviceIdType.MESH
F32, BF16 = jnp.float32, jnp.bfloat16
NEG = -1e30
SURE = 24
PER = 4
WIDE = PER * BLOCK
CHUNKS = R // PER


def dot_nt(a, b):
    return lax.dot_general(a, b, (((1,), (1,)), ((), ())), preferred_element_type=F32)


def dot_nn(a, b):
    return lax.dot_general(a, b, (((1,), (0,)), ((), ())), preferred_element_type=F32)


def dot_tn(a, b):
    return lax.dot_general(a, b, (((0,), (0,)), ((), ())), preferred_element_type=F32)


def kernel(
    owner_ref, block_ref, q_ref, k_ref, v_ref, g_ref, w_ref,
    lo_ref, dq_ref, dk_ref, dv_ref, pg_ref,
    w_v, lo_v, kv, kvc, q4, do4, g4, s_near, p_mem, m_mem, top4, sum4, mix4, stat, attn4, attn_in, lo_out, lo_in,
    pt, pp, rs0, r1, rs2, r2, dq_acc, near_acc, carry_out, carry_in, gq, gk, gv, tab_v, tab,
    loc, ys, yr, gs, gr, xs, xr, zs, zr, ms, mr, as_, ar, bs, br, cs, cr, rzs, rzr, ls, lr, ps, pr, os_, or_,
):
    s_me = lax.axis_index("seg")
    x = lax.axis_index("head")
    c = lax.rem(s_me, NC)
    z = lax.rem(lax.div(s_me, NC), NZ)
    y = lax.div(s_me, NC * NZ)
    scale = 1.0 / math.sqrt(DH)
    scale2 = scale * math.log2(math.e)

    def seg_of(yy, zz, cc):
        return (yy * NZ + zz) * NC + cc

    y_of = [lax.rem(y + d, NY) for d in range(NY)]
    x_of = [lax.rem(x + d, NX) for d in range(NX)]
    z_of = [lax.rem(z + d, NZ) for d in range(NZ)]
    y_peer = [(seg_of(y_of[d], z, c), x) for d in range(NY)]
    z_peer = [(seg_of(y, z_of[d], c), x) for d in range(NZ)]
    x_peer = [(s_me, x_of[d]) for d in range(NX)]
    sibling = (seg_of(y, z, 1 - c), x)
    cross = (seg_of(y, lax.rem(z + NZ - 1 + 2 * c, NZ), 1 - c), x)
    back = (seg_of(y, lax.rem(z + NZ - 1 + c, NZ), 1 - c), x)
    wrap = 1 - jnp.minimum(z + c, 1)

    sends = []

    def send(src, dst, ssem, rsem, dev):
        copy = pltpu.make_async_remote_copy(
            src_ref=src, dst_ref=dst, send_sem=ssem, recv_sem=rsem, device_id=dev, device_id_type=MESH
        )
        copy.start()
        sends.append(copy)

    def arrived(dst, ssem, rsem):
        pltpu.make_async_remote_copy(
            src_ref=dst, dst_ref=dst, send_sem=ssem, recv_sem=rsem, device_id=sibling, device_id_type=MESH
        ).wait_recv()

    def cols(i):
        return pl.ds(pl.multiple_of(i * DH, DH), DH)

    def slot(plane, rz, ry):
        return (plane * NZ + rz) * NY + ry

    own = [
        pltpu.make_async_copy(k_ref.at[:, :, cols(y)], kv.at[0, 0], loc.at[0]),
        pltpu.make_async_copy(v_ref.at[:, :, cols(y)], kv.at[0, 1], loc.at[1]),
        pltpu.make_async_copy(q_ref.at[:, cols(y)], q4.at[0], loc.at[2]),
        pltpu.make_async_copy(g_ref, g4.at[0, x], loc.at[3]),
    ]
    weights_in = pltpu.make_async_copy(w_ref, w_v, loc.at[4])
    for copy in own + [weights_in]:
        copy.start()

    barrier = pltpu.get_barrier_semaphore()
    peers = y_peer[1:] + z_peer[1:] + x_peer[1:] + [sibling, cross]
    for dev in peers:
        pl.semaphore_signal(barrier, inc=1, device_id=dev, device_id_type=MESH)
    pl.semaphore_wait(barrier, len(peers))

    for d in (1, 3, 2):
        send(k_ref.at[:, :, cols(y_of[d])], kv.at[NY - d, 0], ys.at[d - 1, 0], yr.at[NY - d - 1, 0], y_peer[d])
        send(v_ref.at[:, :, cols(y_of[d])], kv.at[NY - d, 1], ys.at[d - 1, 1], yr.at[NY - d - 1, 1], y_peer[d])
    send(g_ref, g4.at[0, x], xs.at[0, 0], xr.at[0, 0], x_peer[1])
    send(g_ref, g4.at[0, x], xs.at[0, 1], xr.at[0, 1], x_peer[NX - 1])
    for copy in own:
        copy.wait()
    order = (0, 1, 3, 2)

    def z_part(t, ry):
        up, down = (NZ - t) % NZ, t
        if t == 0:
            if ry:
                arrived(kv.at[ry, 0], ys.at[ry - 1, 0], yr.at[ry - 1, 0])
                arrived(kv.at[ry, 1], ys.at[ry - 1, 1], yr.at[ry - 1, 1])
        else:
            arrived(kv.at[slot(0, up, ry)], zs.at[0, t - 1, ry], zr.at[0, t - 1, ry])
            arrived(kv.at[slot(0, down, ry)], zs.at[1, t - 1, ry], zr.at[1, t - 1, ry])
        if t < NZ // 2 - 1:
            send(kv.at[slot(0, up, ry)], kv.at[slot(0, NZ - 1 - t, ry)], zs.at[0, t, ry], zr.at[0, t, ry], z_peer[1])
            send(kv.at[slot(0, down, ry)], kv.at[slot(0, t + 1, ry)], zs.at[1, t, ry], zr.at[1, t, ry], z_peer[NZ - 1])
        else:
            far = slot(0, NZ // 2, ry)
            send(kv.at[slot(0, up, ry), 0], kv.at[far, 0], zs.at[0, t, ry], zr.at[0, t, ry], z_peer[1])
            send(kv.at[slot(0, down, ry), 1], kv.at[far, 1], zs.at[1, t, ry], zr.at[1, t, ry], z_peer[NZ - 1])
        for rz in ((0,) if t == 0 else (up, down)):
            send(kv.at[slot(0, rz, ry)], kv.at[slot(1, rz, ry)], ms.at[rz, ry], mr.at[rz, ry], sibling)

    def z_far(ry):
        far, t = slot(0, NZ // 2, ry), NZ // 2 - 1
        arrived(kv.at[far, 0], zs.at[0, t, ry], zr.at[0, t, ry])
        arrived(kv.at[far, 1], zs.at[1, t, ry], zr.at[1, t, ry])
        send(kv.at[far], kv.at[slot(1, NZ // 2, ry)], ms.at[NZ // 2, ry], mr.at[NZ // 2, ry], sibling)

    def take(rz, ry):
        arrived(kv.at[slot(1, rz, ry)], ms.at[rz, ry], mr.at[rz, ry])
        for plane in range(NC):
            kvc[slot(plane, rz, ry)] = kv[slot(plane, rz, ry)]

    def seg_id(ry):
        return seg_of(lax.rem(y + ry, NY), z, c)

    def cache_slot(ry):
        return slot(1, (NZ - 1) * (1 - c), lax.rem(ry + NY - wrap, NY))

    def near(at, which):
        return kvc[at, which].reshape(SEG, DH)

    def fold(m, entry, op):
        for i in range(entry.shape[1] // DH):
            m = op(m, entry[:, i * DH : (i + 1) * DH])
        return m

    def make_table(ry):
        lane = lax.broadcasted_iota(jnp.int32, owner_ref.shape, 1) == seg_id(ry)
        o = jnp.sum(jnp.where(lane, owner_ref[...], 0), axis=1, keepdims=True)
        b = jnp.sum(jnp.where(lane, block_ref[...], 0), axis=1, keepdims=True)
        rz = ((o >> 1) & (NZ - 1)) + NZ - z & (NZ - 1)
        rr = (o >> 4) + NY - y & (NY - 1)
        plane = (o + c) & (NC - 1)
        away = jnp.minimum(rz, NZ - rz)
        dead = b < 0
        turn = rr ^ (rr >> 1)
        stage = jnp.where(away < 3, 0, jnp.where(away == 3, 1 + turn, 1 + NY + turn))
        stage = jnp.where(dead, -1, stage)
        code = jnp.where(dead, 256, ((plane * NZ + rz) * NY + rr) * 2 + jnp.maximum(b, 0))
        down = lax.broadcasted_iota(jnp.int32, (R, R), 0)
        across = lax.broadcasted_iota(jnp.int32, (R, R), 1)
        stage_col = jnp.broadcast_to(stage, (R, R))
        stage_row = jnp.sum(jnp.where(down == across, stage_col, 0), axis=0, keepdims=True)
        first = (stage_row < stage_col) | ((stage_row == stage_col) & (across < down))
        rank = jnp.sum(first.astype(jnp.int32), axis=1, keepdims=True)
        tab_v[ry : ry + 1, :R] = jnp.sum(jnp.where(rank == across, code, 0), axis=0, keepdims=True)

    def stored(ry, i, which):
        parts = []
        for b in range(PER):
            code = tab[ry, i * PER + b]
            parts.append(kvc[(code & 255) >> 1, which, code & 1])
        return jnp.concatenate(parts, axis=0)

    causal = lax.broadcasted_iota(jnp.int32, (SEG, SEG), 0) >= lax.broadcasted_iota(jnp.int32, (SEG, SEG), 1)

    def forward_near(ry):
        q = q4[ry]
        s_own = jnp.where(causal, dot_nt(q, near(ry, 0)), NEG)
        s_near[ry, 0] = s_own
        dead = (1 - jnp.minimum(seg_id(ry), 1)).astype(F32)
        s_cache = dot_nt(q, near(cache_slot(ry), 0)) + dead * NEG
        s_near[ry, 1] = s_cache
        top = fold(fold(s_own[:, :DH], s_own[:, DH:], jnp.maximum), s_cache, jnp.maximum)
        top = jnp.broadcast_to(jnp.max(top, axis=1, keepdims=True), (SEG, DH))
        total = jnp.zeros((SEG, DH), F32)
        mixed = jnp.zeros((SEG, DH), F32)
        wide_top = jnp.concatenate([top] * (SEG // DH), axis=1)
        for s, at in ((s_own, ry), (s_cache, cache_slot(ry))):
            p = jnp.exp2((s - wide_top) * scale2)
            total = fold(total, p, jnp.add)
            mixed += dot_nn(p.astype(BF16), near(at, 1))
        top4[ry], sum4[ry], mix4[ry] = top, total, mixed

    def forward_mem(i):
        def pair(n, _):
            rys = [n * 2, n * 2 + 1]
            scores = [dot_nt(q4[ry], stored(ry, i, 0)) for ry in rys]
            for ry, s in zip(rys, scores):
                if i * PER < R - SURE:
                    parts = []
                    for b in range(PER):
                        dead = (tab[ry, i * PER + b] >> 8).astype(F32)
                        parts.append(s[:, b * BLOCK : (b + 1) * BLOCK] + dead * NEG)
                    s = jnp.concatenate(parts, axis=1)
                old = top4[ry]
                top = jnp.max(fold(s[:, :DH], s[:, DH:], jnp.maximum), axis=1, keepdims=True)
                top = jnp.maximum(old, jnp.broadcast_to(top, (SEG, DH)))
                less = jnp.exp2((old - top) * scale2)
                p = jnp.exp2((s - jnp.concatenate([top] * (WIDE // DH), axis=1)) * scale2)
                sum4[ry] = fold(sum4[ry] * less, p, jnp.add)
                p = p.astype(BF16)
                p_mem[ry, i] = p
                mix4[ry] = mix4[ry] * less + dot_nn(p, stored(ry, i, 1))
                top4[ry] = top
                m_mem[ry, i] = top
            return _

        lax.fori_loop(0, NY // 2, pair, 0)

    def finish(ry):
        inv = 1.0 / jnp.sum(sum4[ry], axis=1, keepdims=True)
        attn = (mix4[ry] * inv).astype(BF16)
        attn4[ry] = attn
        delta = jnp.sum(do4[ry].astype(F32) * attn.astype(F32), axis=1, keepdims=True)
        stat[ry, 0] = top4[ry]
        stat[ry, 1] = jnp.broadcast_to(inv, (SEG, DH))
        stat[ry, 2] = jnp.broadcast_to(delta, (SEG, DH))

    lower, upper = pl.ds(0, SEG // 2), pl.ds(SEG // 2, SEG // 2)
    width = g4.shape[3]

    def x_first(ry):
        arrived(g4.at[ry, x], gs.at[ry - 1], gr.at[ry - 1])
        send(g4.at[ry, x], g4.at[ry, x], xs.at[ry, 0], xr.at[ry, 0], x_peer[1])
        send(g4.at[ry, x], g4.at[ry, x], xs.at[ry, 1], xr.at[ry, 1], x_peer[NX - 1])

    def x_second(ry):
        left, right = x_of[NX - 1], x_of[1]
        arrived(g4.at[ry, left], xs.at[ry, 0], xr.at[ry, 0])
        send(g4.at[ry, left, lower], g4.at[ry, left, lower], xs.at[ry, 2], xr.at[ry, 2], x_peer[1])
        arrived(g4.at[ry, right], xs.at[ry, 1], xr.at[ry, 1])
        send(g4.at[ry, right, upper], g4.at[ry, right, upper], xs.at[ry, 3], xr.at[ry, 3], x_peer[NX - 1])

    def d_attn(ry):
        arrived(g4.at[ry, x_of[2], lower], xs.at[ry, 2], xr.at[ry, 2])
        arrived(g4.at[ry, x_of[2], upper], xs.at[ry, 3], xr.at[ry, 3])
        da = jnp.zeros((SEG, DH), F32)
        for i in range(NX):
            da += dot_nt(g4[ry, i], w_v[cols(y), i * width : (i + 1) * width])
        do4[ry] = da.astype(BF16)

    def g_send(d):
        send(g_ref, g4.at[NY - d, x], gs.at[d - 1], gr.at[NY - d - 1], y_peer[d])

    z_part(0, 0)
    z_part(1, 0)
    z_part(0, 1)
    z_part(0, 3)
    for d in (3, 1, 2):
        g_send(d)
    x_second(0)
    z_part(0, 2)
    for d in (1, 3, 2):
        send(q_ref.at[:, cols(y_of[d])], q4.at[NY - d], ys.at[d - 1, 2], yr.at[NY - d - 1, 2], y_peer[d])
    z_part(2, 0)
    for ry in range(NY):
        make_table(ry)
    to_smem = pltpu.make_async_copy(tab_v, tab, loc.at[0])
    to_smem.start()
    z_part(1, 1)
    weights_in.wait()
    z_part(1, 3)
    d_attn(0)
    z_part(1, 2)
    x_first(1)
    x_first(3)
    to_smem.wait()
    for ry in range(1, NY):
        arrived(q4.at[ry], ys.at[ry - 1, 2], yr.at[ry - 1, 2])
    for ry in order:
        take(0, ry)
    for ry in order:
        take(NZ - 1, ry)

    def near_step(ry, _):
        forward_near(ry)
        return _

    lax.fori_loop(0, NY, near_step, 0)
    z_part(3, 0)
    z_part(2, 1)
    x_first(2)
    z_part(2, 3)
    x_second(1)
    for ry in order:
        take(1, ry)
    z_part(2, 2)
    for rz in (NZ - 2, 2):
        for ry in order:
            take(rz, ry)
    forward_mem(0)
    x_second(3)
    z_far(0)
    forward_mem(1)
    take(NZ - 3, 0)
    take(3, 0)
    z_part(3, 1)
    forward_mem(2)
    take(NZ - 3, 1)
    take(3, 1)
    z_part(3, 3)
    forward_mem(3)
    take(NZ - 3, 3)
    take(3, 3)
    x_second(2)
    d_attn(1)
    z_part(3, 2)
    forward_mem(4)
    take(NZ - 3, 2)
    take(3, 2)
    z_far(1)
    forward_mem(5)
    take(NZ // 2, 0)
    take(NZ // 2, 1)
    z_far(3)
    d_attn(3)
    z_far(2)
    forward_mem(6)
    d_attn(2)
    take(NZ // 2, 3)
    take(NZ // 2, 2)
    forward_mem(7)

    def backward_near(ry):
        q, do = q4[ry], do4[ry]
        top, inv, delta = stat[ry, 0, :, :1], stat[ry, 1, :, :1], stat[ry, 2, :, :1]
        dq = jnp.zeros((SEG, DH), F32)
        for part, at in ((0, ry), (1, cache_slot(ry))):
            weights = jnp.exp2((s_near[ry, part] - top) * scale2) * inv
            slopes = (weights * (dot_nt(do, near(at, 1)) - delta)).astype(BF16)
            dq += dot_nn(slopes, near(at, 0))
            gk_part = dot_tn(slopes, q) * scale
            gv_part = dot_tn(weights.astype(BF16), do)
            if part == 0:
                near_acc[ry, 0] = gk_part
                near_acc[ry, 1] = gv_part
            else:
                carry_out[ry, 0] = gk_part.astype(BF16)
                carry_out[ry, 1] = gv_part.astype(BF16)
        dq_acc[ry] = dq

    def backward_mem(ry):
        do = do4[ry]
        top, inv, delta = stat[ry, 0], stat[ry, 1], stat[ry, 2]
        wide_delta = jnp.concatenate([delta] * (WIDE // DH), axis=1)

        def step(n, dq):
            for i in [4 * n + k for k in range(4)]:
                slopes = (p_mem[ry, i].astype(F32) * (dot_nt(do, stored(ry, i, 1)) - wide_delta)).astype(BF16)
                dq += dot_nn(slopes, stored(ry, i, 0)) * jnp.exp2((m_mem[ry, i] - top) * scale2)
            return dq

        dq = lax.fori_loop(0, CHUNKS // 4, step, jnp.zeros((SEG, DH), F32))
        gq[ry] = ((dq_acc[ry] + dq * inv) * scale).astype(BF16)

    for n, ry in enumerate((2, 1, 3, 0)):
        finish(ry)
        if ry:
            send(attn4.at[ry], attn_in.at[y], as_.at[ry - 1], ar.at[ry - 1], y_peer[ry])
        turned = attn4[ry].T
        for i in range(NX):
            part = dot_nn(turned, g4[ry, i])
            pt[i] = part if n == 0 else pt[i] + part
    attn_in[y] = attn4[0]

    rows = pg_ref.shape[0]
    for i in range(NY):
        pp[i] = pt[i].T.astype(BF16).reshape(NZ, NC, rows, DH)
        send(pp.at[i, :, 1 - c], rs0.at[i], bs.at[i], br.at[i], sibling)

    def near_and_carry(ry):
        backward_near(ry)
        to = lax.rem(ry + NY - wrap, NY)
        send(carry_out.at[ry], carry_in.at[to], cs.at[ry], cr.at[to], back)

    near_and_carry(0)
    near_and_carry(1)
    for i in range(NY):
        arrived(rs0.at[i], bs.at[i], br.at[i])
        r1[:, i] = (pp[i, :, c].astype(F32) + rs0[i].astype(F32)).astype(BF16)
    for d in (4, 3, 5, 2, 6, 1, 7):
        send(r1.at[z_of[d]], rs2.at[d - 1], rzs.at[d - 1], rzr.at[d - 1], z_peer[d])
    near_and_carry(2)
    near_and_carry(3)

    for d in (1, 3, 2):
        arrived(attn_in.at[y_of[NY - d]], as_.at[d - 1], ar.at[d - 1])
    attn = jnp.concatenate([attn_in[i] for i in range(NY)], axis=1)
    for i in range(NX):
        lo_out[i] = dot_nn(attn, w_v[:, i * width : (i + 1) * width]).astype(BF16)
    for d in (2, 1, 3):
        send(lo_out.at[x_of[d]], lo_in.at[d - 1], ls.at[d - 1], lr.at[d - 1], x_peer[d])
    backward_mem(2)
    send(gq.at[2], dq_ref.at[:, cols(y)], os_.at[0, 1], or_.at[0, 1], y_peer[2])
    for ry in (2, 1, 3, 0):
        arrived(carry_in.at[ry], cs.at[ry], cr.at[ry])
        gk[ry] = (near_acc[ry, 0] + carry_in[ry, 0].astype(F32)).astype(BF16)
        gv[ry] = (near_acc[ry, 1] + carry_in[ry, 1].astype(F32)).astype(BF16)
        if ry:
            send(gk.at[ry], dk_ref.at[:, cols(y)], os_.at[1, ry - 1], or_.at[1, ry - 1], y_peer[ry])
            send(gv.at[ry], dv_ref.at[:, cols(y)], os_.at[2, ry - 1], or_.at[2, ry - 1], y_peer[ry])
    backward_mem(1)
    send(gq.at[1], dq_ref.at[:, cols(y)], os_.at[0, 0], or_.at[0, 0], y_peer[1])
    total = r1[z].astype(F32)
    for d in range(1, NZ):
        arrived(rs2.at[d - 1], rzs.at[d - 1], rzr.at[d - 1])
        total += rs2[d - 1].astype(F32)
    r2[...] = total
    for d in (2, 1, 3):
        send(r2.at[y_of[d]], pg_ref.at[:, cols(y)], ps.at[d - 1], pr.at[d - 1], y_peer[d])
    backward_mem(3)
    send(gq.at[3], dq_ref.at[:, cols(y)], os_.at[0, 2], or_.at[0, 2], y_peer[3])
    backward_mem(0)

    home = [
        pltpu.make_async_copy(gq.at[0], dq_ref.at[:, cols(y)], loc.at[0]),
        pltpu.make_async_copy(gk.at[0], dk_ref.at[:, cols(y)], loc.at[1]),
        pltpu.make_async_copy(gv.at[0], dv_ref.at[:, cols(y)], loc.at[2]),
        pltpu.make_async_copy(r2.at[y], pg_ref.at[:, cols(y)], loc.at[5]),
    ]
    for copy in home:
        copy.start()
    out = lo_out[x].astype(F32)
    for d in range(1, NX):
        arrived(lo_in.at[d - 1], ls.at[d - 1], lr.at[d - 1])
        out += lo_in[d - 1].astype(F32)
    lo_v[...] = out.astype(BF16)
    home.append(pltpu.make_async_copy(lo_v, lo_ref, loc.at[3]))
    home[-1].start()
    for d in range(1, NY):
        arrived(pg_ref.at[:, cols(y_of[NY - d])], ps.at[d - 1], pr.at[d - 1])
    for n, ref in enumerate((dq_ref, dk_ref, dv_ref)):
        for d in range(1, NY):
            arrived(ref.at[:, cols(y_of[NY - d])], os_.at[n, d - 1], or_.at[n, d - 1])
    for copy in home:
        copy.wait()
    for copy in sends:
        copy.wait_send()


def hand_over(*refs):
    for i in range(5):
        refs[5 + i][...] = refs[i][...]


def per_device(queries, keys, values, out_grad, out_weight, retr_owner, retr_block):
    tok, wide = queries.shape
    full = out_weight.shape[1]
    rows = full // (NY * NZ * NC)
    vmem = pl.BlockSpec(memory_space=pltpu.VMEM)
    anywhere = pl.BlockSpec(memory_space=pl.ANY)
    dma = pltpu.SemaphoreType.DMA
    tile = (tok, DH)
    halves = tok // BLOCK
    scratch = [
        pltpu.VMEM((wide, full), BF16),
        pltpu.VMEM((tok, wide), BF16),
        pltpu.VMEM((NC * NZ * NY, 2, halves, BLOCK, DH), BF16),
        pltpu.VMEM((NC * NZ * NY, 2, halves, BLOCK, DH), BF16),
        pltpu.VMEM((NY,) + tile, BF16),
        pltpu.VMEM((NY,) + tile, BF16),
        pltpu.VMEM((NY, NX, tok, wide), BF16),
        pltpu.VMEM((NY, 2, tok, tok), F32),
        pltpu.VMEM((NY, CHUNKS, tok, WIDE), BF16),
        pltpu.VMEM((NY, CHUNKS) + tile, F32),
        pltpu.VMEM((NY,) + tile, F32),
        pltpu.VMEM((NY,) + tile, F32),
        pltpu.VMEM((NY,) + tile, F32),
        pltpu.VMEM((NY, 3) + tile, F32),
        pltpu.VMEM((NY,) + tile, BF16),
        pltpu.VMEM((NY,) + tile, BF16),
        pltpu.VMEM((NX, tok, wide), BF16),
        pltpu.VMEM((NX - 1, tok, wide), BF16),
        pltpu.VMEM((NX, DH, wide), F32),
        pltpu.VMEM((NY, NZ, NC, rows, DH), BF16),
        pltpu.VMEM((NY, NZ, rows, DH), BF16),
        pltpu.VMEM((NZ, NY, rows, DH), BF16),
        pltpu.VMEM((NZ - 1, NY, rows, DH), BF16),
        pltpu.VMEM((NY, rows, DH), F32),
        pltpu.VMEM((NY,) + tile, F32),
        pltpu.VMEM((NY, 2) + tile, F32),
        pltpu.VMEM((NY, 2) + tile, BF16),
        pltpu.VMEM((NY, 2) + tile, BF16),
        pltpu.VMEM((NY,) + tile, BF16),
        pltpu.VMEM((NY,) + tile, BF16),
        pltpu.VMEM((NY,) + tile, BF16),
        pltpu.VMEM((8, DH), jnp.int32),
        pltpu.SMEM((8, DH), jnp.int32),
        dma((6,)),
        dma((NY - 1, 3)), dma((NY - 1, 3)),
        dma((NY - 1,)), dma((NY - 1,)),
        dma((NY, 4)), dma((NY, 4)),
        dma((2, NZ // 2, NY)), dma((2, NZ // 2, NY)),
        dma((NZ, NY)), dma((NZ, NY)),
        dma((NY - 1,)), dma((NY - 1,)),
        dma((NY,)), dma((NY,)),
        dma((NY,)), dma((NY,)),
        dma((NZ - 1,)), dma((NZ - 1,)),
        dma((NX - 1,)), dma((NX - 1,)),
        dma((NY - 1,)), dma((NY - 1,)),
        dma((3, NY - 1)), dma((3, NY - 1)),
    ]
    grad = jax.ShapeDtypeStruct((tok, wide), BF16)
    shapes = (grad, grad, grad, grad, jax.ShapeDtypeStruct((rows, wide), F32))
    results = pl.pallas_call(
        kernel,
        out_shape=shapes,
        in_specs=[vmem] * 2 + [anywhere] * 5,
        out_specs=(anywhere,) * 5,
        scratch_shapes=scratch,
        compiler_params=pltpu.CompilerParams(
            collective_id=0, has_side_effects=True, vmem_limit_bytes=60 * 1024 * 1024
        ),
    )(
        retr_owner.T,
        retr_block.T,
        queries,
        keys.reshape(halves, BLOCK, wide),
        values.reshape(halves, BLOCK, wide),
        out_grad,
        out_weight,
    )
    return pl.pallas_call(hand_over, out_shape=shapes, in_specs=[vmem] * 5, out_specs=(vmem,) * 5)(*results)


def solution(mesh):
    rows = P("seg", "head")
    return jax.shard_map(
        per_device,
        mesh=mesh,
        in_specs=(rows, rows, rows, rows, P("head", None), P(), P()),
        out_specs=(rows,) * 5,
        check_vma=False,
    )
```
